256 devices in a mesh: fsdp: 16 (over y_lo, z), dp: 8 (over x, core), query: 2 (over y_hi).
Axes of the slice: x: 4, y: 4 (y_hi: 2, y_lo: 2; y = y_hi * 2 + y_lo), z: 8, core: 2. Of those that a mesh axis runs over, the one named last changes fastest.
Arguments:
- doc_inputs: bfloat16 [256, 32, 5120], P(('fsdp', 'query')), may hold values from -6 to 6
- doc_cotangents: bfloat16 [256, 32, 7168], P(('fsdp', 'query'), None, 'dp'), may hold values from -6 to 6
- query_inputs: bfloat16 [256, 32, 5120], P(('fsdp', 'query')), may hold values from -6 to 6
- query_cotangents: bfloat16 [256, 32, 7168], P(('fsdp', 'query'), None, 'dp'), may hold values from -6 to 6
- gate_weight: bfloat16 [5120, 7168], P('fsdp', ('dp', 'query')), may hold values from -0.078125 to 0.078125
- up_weight: bfloat16 [5120, 7168], P('fsdp', ('dp', 'query')), may hold values from -0.078125 to 0.078125
- input_projection: bfloat16 [64, 5120], replicated, may hold values from -0.078125 to 0.078125
- gate_projection: bfloat16 [64, 7168], P(None, 'dp'), may hold values from -0.0625 to 0.0625
- up_projection: bfloat16 [64, 7168], P(None, 'dp'), may hold values from -0.0625 to 0.0625
Outputs:
- influence: float32 [32, 8, 256], P(('fsdp', 'query'), 'dp')
The draws below stay inside these ranges and needn't reach their ends.
All inputs are finite; a program needn't handle non-finite values.
Results may differ from the reference program's by a relative error of at most 0.0057.
Values may be sent and summed in bfloat16 or wider, within the bound.
No kernel may reach another device: no remote copies, remote signals or barrier semaphores. Data moves between devices by JAX's collectives and lax.ppermute only.
A program may use at most 128 MiB of HBM per device.

```python
import jax
import jax.numpy as jnp
from jax import lax

D = 5120
FFW = 7168
RANK = 64
LEN = 32
QLEN = 32
GROUPS = 32
DOCS_G = 8
QRY_G = 8
DOCS = 256
QUERIES = 256


def block_levels(stream_key, extent, split, low, high):
    level, own = 1.0, jax.random.fold_in(stream_key, 6)
    for position, blocks in split:
        heights = jnp.exp(jax.random.uniform(jax.random.fold_in(own, position), (blocks,), jnp.float32, low / len(split), high / len(split)))
        level = level * jnp.repeat(heights, extent[position] // blocks).reshape([-1 if axis == position else 1 for axis in range(len(extent))])
    return level


def centred(rng, extent, scale, most, shards=(), held_as=jnp.bfloat16):
    loudness = block_levels(rng, extent, shards, -0.22, 0.18) if shards else 1.0
    drawn = jax.random.normal(rng, extent, jnp.float32) * scale * loudness
    return jnp.minimum(jnp.maximum(drawn, -most), most).astype(held_as)


def setup_inputs(seed: int = 0) -> dict:
    key_list = jax.random.split(jax.random.key(seed), 10)
    doc_inputs = centred(key_list[0], (DOCS, LEN, D), 1.0, 6.0, ((0, 32),))
    doc_cotangents = centred(key_list[1], (DOCS, LEN, FFW), 1.0, 6.0, ((0, 32), (2, 8)))
    query_inputs = centred(key_list[2], (QUERIES, QLEN, D), 1.0, 6.0, ((0, 32),))
    query_cotangents = centred(key_list[3], (QUERIES, QLEN, FFW), 1.0, 6.0, ((0, 32), (2, 8)))
    gate_weight = centred(key_list[4], (D, FFW), D ** -0.5, 0.078125, ((0, 16), (1, 16)))
    up_weight = centred(key_list[5], (D, FFW), D ** -0.5, 0.078125, ((0, 16), (1, 16)))
    input_projection = centred(key_list[6], (RANK, D), D ** -0.5, 0.078125)
    gate_projection = centred(key_list[7], (RANK, FFW), FFW ** -0.5, 0.0625, ((1, 8),))
    up_projection = centred(key_list[8], (RANK, FFW), FFW ** -0.5, 0.0625, ((1, 8),))
    return {"doc_inputs": doc_inputs, "doc_cotangents": doc_cotangents, "query_inputs": query_inputs, "query_cotangents": query_cotangents, "gate_weight": gate_weight, "up_weight": up_weight, "input_projection": input_projection, "gate_projection": gate_projection, "up_projection": up_projection}


def example_units(inputs, cotangents, gate_weight, up_weight, input_projection, gate_projection, up_projection):
    count, length, width = inputs.shape
    rows = inputs.reshape(count * length, width)
    gate = jnp.dot(rows, gate_weight, preferred_element_type=jnp.float32)
    up = jnp.dot(rows, up_weight, preferred_element_type=jnp.float32)
    sigma = jax.nn.sigmoid(gate)
    upstream = cotangents.reshape(count * length, -1).astype(jnp.float32)
    gate_grad = (upstream * up * sigma * (1.0 + gate * (1.0 - sigma))).astype(jnp.bfloat16)
    up_grad = (upstream * gate * sigma).astype(jnp.bfloat16)
    out_factor = jnp.concatenate((jnp.dot(gate_grad, gate_projection.T, preferred_element_type=jnp.float32), jnp.dot(up_grad, up_projection.T, preferred_element_type=jnp.float32)), axis=1)
    in_factor = jnp.dot(rows, input_projection.T, preferred_element_type=jnp.float32)
    factors = jnp.einsum('elr,elk->erk', in_factor.reshape(count, length, -1), out_factor.reshape(count, length, -1), precision=lax.Precision.HIGHEST)
    flat = factors.reshape(count, -1)
    scale = jnp.sqrt(lax.optimization_barrier(jnp.mean(flat * flat, axis=1, keepdims=True)) + 1e-06)
    return (flat / scale).astype(jnp.bfloat16)

def reference(doc_inputs, doc_cotangents, query_inputs, query_cotangents, gate_weight, up_weight, input_projection, gate_projection, up_projection):

    def units_of(pair):
        return example_units(pair[0], pair[1], gate_weight, up_weight, input_projection, gate_projection, up_projection)
    doc_units = lax.map(units_of, (doc_inputs.reshape(GROUPS, DOCS_G, LEN, D), doc_cotangents.reshape(GROUPS, DOCS_G, LEN, FFW))).reshape(DOCS, -1)
    query_units = lax.map(units_of, (query_inputs.reshape(GROUPS, QRY_G, QLEN, D), query_cotangents.reshape(GROUPS, QRY_G, QLEN, FFW))).reshape(QUERIES, -1)
    scores = jnp.dot(doc_units, query_units.T, preferred_element_type=jnp.float32) / RANK
    return scores.reshape(GROUPS, DOCS_G, QUERIES)
```

```python
import jax
import jax.numpy as jnp
from jax import lax
from jax.sharding import PartitionSpec as P

F32 = jnp.float32
BF16 = jnp.bfloat16
SWAP = ((0, 1), (1, 0))


def ring_perm(size, inner, step):
    outer = size // inner
    return [
        (o * inner + i, o * inner + (i + step) % inner)
        for o in range(outer)
        for i in range(inner)
    ]


def x_shift(value, chips, step):
    perm = [
        (x * 2 + c, ((x + step) % chips) * 2 + c) for x in range(chips) for c in range(2)
    ]
    return lax.ppermute(value, "dp", perm)


def core_swap(value, size):
    return lax.ppermute(value, "dp", [(i, i ^ 1) for i in range(size)])


def partner_rows(rows):
    size = lax.axis_size("dp")
    chips = size // 2
    place = lax.axis_index("dp")
    chip, core = place // 2, place % 2
    mine = lax.dynamic_slice_in_dim(rows, place, 1, 0)
    here = lax.ppermute(mine, "query", SWAP)
    half = rows.shape[1] // 2
    left = x_shift(here, chips, 1)
    right = x_shift(here, chips, -1)
    far_a = x_shift(left[:, :half], chips, 1)
    far_b = x_shift(right[:, half:], chips, -1)
    far = jnp.concatenate((far_a, far_b), axis=1)
    result = jnp.zeros_like(rows)
    for offset, piece in ((0, here), (-1, left), (1, right), (2, far)):
        other = core_swap(piece, size)
        owner = (chip + offset + chips) % chips
        result = lax.dynamic_update_slice(result, piece, (owner * 2 + core, 0, 0))
        result = lax.dynamic_update_slice(result, other, (owner * 2 + 1 - core, 0, 0))
    return result


def projected(pre, cotangent, gate_projection, up_projection):
    cols = pre.shape[1] // 2
    gate = pre[:, :cols]
    up = pre[:, cols:]
    sigma = jax.nn.sigmoid(gate)
    upstream = cotangent.astype(F32)
    gate_grad = (upstream * up * sigma * (1.0 + gate * (1.0 - sigma))).astype(BF16)
    up_grad = (upstream * gate * sigma).astype(BF16)
    dims = (((1,), (1,)), ((), ()))
    return jnp.concatenate(
        (
            lax.dot_general(gate_projection, gate_grad, dims, preferred_element_type=F32),
            lax.dot_general(up_projection, up_grad, dims, preferred_element_type=F32),
        ),
        axis=0,
    )


def body(
    doc_inputs,
    doc_cotangents,
    query_inputs,
    query_cotangents,
    gate_weight,
    up_weight,
    input_projection,
    gate_projection,
    up_projection,
):
    count, length, width = doc_inputs.shape
    half_index = lax.axis_index("query")
    dq = ("dp", "query")
    n_dq = lax.axis_size("dp") * lax.axis_size("query")
    n_fsdp = lax.axis_size("fsdp")
    rank = input_projection.shape[0]

    weight = jnp.concatenate((gate_weight, up_weight), axis=1)
    weight = lax.all_gather(weight, "fsdp", axis=0, tiled=True)
    cols = gate_weight.shape[1]

    own = jnp.concatenate((doc_inputs, query_inputs), axis=1)
    other = partner_rows(own)
    cot = jnp.concatenate((doc_cotangents, query_cotangents), axis=1)
    cot = cot.reshape(-1, cot.shape[2])
    own_cot = lax.dynamic_slice_in_dim(cot, half_index * cols, cols, 1)
    other_cot = lax.ppermute(
        lax.dynamic_slice_in_dim(cot, (1 - half_index) * cols, cols, 1), "query", SWAP
    )
    gate_proj = lax.dynamic_slice_in_dim(gate_projection, half_index * cols, cols, 1)
    up_proj = lax.dynamic_slice_in_dim(up_projection, half_index * cols, cols, 1)

    parts = []
    factors = []
    for rows, rows_cot in ((own, own_cot), (other, other_cot)):
        flat = rows.reshape(-1, width)
        pre = jnp.dot(flat, weight, preferred_element_type=F32)
        parts.append(projected(pre, rows_cot, gate_proj, up_proj))
        factors.append(
            lax.dot_general(
                flat, input_projection, (((1,), (1,)), ((), ())), preferred_element_type=F32
            )
        )

    first = half_index == 0

    def ordered(pair, axis):
        a = jnp.where(first, pair[0], pair[1])
        b = jnp.where(first, pair[1], pair[0])
        return jnp.concatenate((a, b), axis=axis)

    part = ordered(parts, 1).astype(BF16)
    in_factor = ordered(factors, 0)
    ranks = part.shape[0] // n_dq
    part = part.reshape(n_dq, ranks, -1)
    swapped = lax.all_to_all(part, dq, 0, 0, tiled=True)
    out_sum = jnp.sum(swapped.astype(F32), axis=0)

    pairs = 2 * count
    factor = jnp.einsum(
        "kel,elr->ekr",
        out_sum.reshape(ranks, 2 * pairs, length),
        in_factor.reshape(2 * pairs, length, rank),
        precision=lax.Precision.HIGHEST,
    ).reshape(pairs, 2, ranks * rank)
    docs = factor[:, 0]
    queries = factor[:, 1]
    doc_squares = jnp.sum(docs * docs, axis=1)
    docs = docs.astype(BF16)
    queries = queries.astype(BF16)

    everyone = lax.all_to_all(
        jnp.broadcast_to(queries[None], (n_fsdp,) + queries.shape), "fsdp", 0, 0, tiled=True
    ).reshape(n_fsdp * pairs, -1)
    wide = everyone.astype(F32)
    query_squares = jnp.sum(wide * wide, axis=1)
    scores = lax.dot_general(
        docs, everyone, (((1,), (1,)), ((), ())), preferred_element_type=F32
    )
    total = scores.shape[1]

    def to_destinations(x):
        return x.reshape((2, count) + x.shape[1:]).swapaxes(0, 1).reshape(x.shape)

    payload = jnp.concatenate(
        (
            to_destinations(scores),
            jnp.broadcast_to(query_squares[None], (pairs, total)),
            jnp.broadcast_to(to_destinations(doc_squares)[:, None], (pairs, 128)),
        ),
        axis=1,
    )
    received = lax.all_to_all(payload, dq, 0, 0, tiled=True)
    sums = jnp.sum(received, axis=0)
    entries = 1.0 / (rank * 2 * rank)
    doc_scale = lax.rsqrt(sums[2 * total] * entries + 1e-06)
    query_scale = lax.rsqrt(sums[total : 2 * total] * entries + 1e-06)
    result = sums[:total] * query_scale * (doc_scale / rank)
    return result.reshape(1, 1, total)


def solution(mesh):
    return jax.shard_map(
        body,
        mesh=mesh,
        in_specs=(
            P(("fsdp", "query"), None, None),
            P(("fsdp", "query"), None, "dp"),
            P(("fsdp", "query"), None, None),
            P(("fsdp", "query"), None, "dp"),
            P("fsdp", ("dp", "query")),
            P("fsdp", ("dp", "query")),
            P(),
            P(None, "dp"),
            P(None, "dp"),
        ),
        out_specs=P(("fsdp", "query"), "dp", None),
        check_vma=False,
    )
```

```python
import jax
import jax.numpy as jnp
from jax import lax
from jax.sharding import PartitionSpec as P

F32 = jnp.float32
BF16 = jnp.bfloat16

def shift(value, axis, step):
    size = lax.axis_size(axis)
    return lax.ppermute(value, axis, [(i, (i + step) % size) for i in range(size)])


def gathered(weight, cot, rows):
    barrier = lax.optimization_barrier
    n_z = lax.axis_size("z")
    n_x = lax.axis_size("x")
    z = lax.axis_index("z")
    chip = lax.axis_index("x")
    core = lax.axis_index("core")
    half = weight.shape[0] // 2

    def up(value):
        return shift(value, "z", 1)

    def down(value):
        return shift(value, "z", -1)

    def across(value):
        return shift(value, "ylo", 1)

    mine = lax.dynamic_slice_in_dim(rows, chip * 2 + core, 1, 0)
    a1, b1, here, w0 = barrier((up(weight), down(weight), shift(mine, "yhi", 1), weight))
    left, right, far = shift(here, "x", 1), shift(here, "x", -1), shift(here, "x", 2)
    a2, b2, o0 = barrier((up(a1), down(b1), across(w0)))
    a3, b3, oa2, o0, b2, left, right, far = barrier(
        (up(a2), down(b2), across(a2), o0, b2, left, right, far)
    )
    pieces = jnp.concatenate((here, left, right, far), axis=0)
    oa1, ob1, ob2, others, a3, b3, oa2 = barrier(
        (up(o0), down(o0), across(b2), shift(pieces, "core", 1), a3, b3, oa2)
    )
    up_pair = up(jnp.concatenate((oa2, a3[:half]), axis=0))
    down_pair = down(jnp.concatenate((ob2, b3[half:]), axis=0))
    up_pair, down_pair, cot = barrier((up_pair, down_pair, shift(cot, "yhi", 1)))
    full = 2 * half
    oa3, a4 = up_pair[:full], up_pair[full:]
    ob3, b4 = down_pair[:full], down_pair[full:]
    oa4 = up(oa3[:half])
    ob4 = down(ob3[half:])

    def placed(by_offset, high, low):
        result = jnp.zeros((n_z,) + weight.shape, weight.dtype)
        for offset, shard in by_offset:
            result = lax.dynamic_update_slice(result, shard[None], ((z + offset) % n_z, 0, 0))
        far_z = (z + n_z // 2) % n_z
        result = lax.dynamic_update_slice(result, high[None], (far_z, 0, 0))
        result = lax.dynamic_update_slice(result, low[None], (far_z, half, 0))
        return result.reshape(n_z * full, -1)

    this_row = placed(
        ((0, w0), (n_z - 1, a1), (1, b1), (n_z - 2, a2), (2, b2), (n_z - 3, a3), (3, b3)), a4, b4
    )
    other_row = placed(
        ((0, o0), (n_z - 1, oa1), (1, ob1), (n_z - 2, oa2), (2, ob2), (n_z - 3, oa3), (3, ob3)),
        oa4,
        ob4,
    )
    partner = jnp.zeros_like(rows)
    for index, offset in enumerate((0, n_x - 1, 1, 2)):
        owner = ((chip + offset) % n_x) * 2
        partner = lax.dynamic_update_slice(
            partner, pieces[index : index + 1], (owner + core, 0, 0)
        )
        partner = lax.dynamic_update_slice(
            partner, others[index : index + 1], (owner + 1 - core, 0, 0)
        )
    return this_row, other_row, cot, partner


def projected(pre, cotangent, gate_projection, up_projection):
    cols = pre.shape[1] // 2
    gate = pre[:, :cols]
    up = pre[:, cols:]
    sigma = jax.nn.sigmoid(gate)
    upstream = cotangent.astype(F32)
    gate_grad = (upstream * up * sigma * (1.0 + gate * (1.0 - sigma))).astype(BF16)
    up_grad = (upstream * gate * sigma).astype(BF16)
    dims = (((1,), (1,)), ((), ()))
    return jnp.concatenate(
        (
            lax.dot_general(gate_projection, gate_grad, dims, preferred_element_type=F32),
            lax.dot_general(up_projection, up_grad, dims, preferred_element_type=F32),
        ),
        axis=0,
    )


def body(
    doc_inputs,
    doc_cotangents,
    query_inputs,
    query_cotangents,
    gate_weight,
    up_weight,
    input_projection,
    gate_projection,
    up_projection,
):
    count, length, width = doc_inputs.shape
    half_index = lax.axis_index("yhi")
    row_index = lax.axis_index("ylo")
    dq = ("x", "core", "yhi")
    fsdp = ("ylo", "z")
    n_dq = lax.axis_size(dq)
    n_fsdp = lax.axis_size(fsdp)
    rank = input_projection.shape[0]
    cols = gate_weight.shape[1]

    own = jnp.concatenate((doc_inputs, query_inputs), axis=1)
    cot = jnp.concatenate((doc_cotangents, query_cotangents), axis=1)
    cot = cot.reshape(-1, cot.shape[2])
    own_cot = lax.dynamic_slice_in_dim(cot, half_index * cols, cols, 1)
    sent_cot = lax.dynamic_slice_in_dim(cot, (1 - half_index) * cols, cols, 1)
    weight = jnp.concatenate((gate_weight, up_weight), axis=1)
    this_row, other_row, other_cot, other = gathered(weight, sent_cot, own)
    gate_proj = lax.dynamic_slice_in_dim(gate_projection, half_index * cols, cols, 1)
    up_proj = lax.dynamic_slice_in_dim(up_projection, half_index * cols, cols, 1)

    parts = []
    factors = []
    depth = this_row.shape[0]
    for rows, rows_cot in ((own, own_cot), (other, other_cot)):
        flat = rows.reshape(-1, width)
        this_flat = lax.dynamic_slice_in_dim(flat, row_index * depth, depth, 1)
        other_flat = lax.dynamic_slice_in_dim(flat, (1 - row_index) * depth, depth, 1)
        pre = jnp.dot(this_flat, this_row, preferred_element_type=F32)
        pre = pre + jnp.dot(other_flat, other_row, preferred_element_type=F32)
        parts.append(projected(pre, rows_cot, gate_proj, up_proj))
        factors.append(
            lax.dot_general(
                flat, input_projection, (((1,), (1,)), ((), ())), preferred_element_type=F32
            )
        )

    first = half_index == 0

    def ordered(pair, axis):
        a = jnp.where(first, pair[0], pair[1])
        b = jnp.where(first, pair[1], pair[0])
        return jnp.concatenate((a, b), axis=axis)

    part = ordered(parts, 1).astype(BF16)
    in_factor = ordered(factors, 0)
    ranks = part.shape[0] // n_dq
    part = part.reshape(n_dq, ranks, -1)
    swapped = lax.all_to_all(part, dq, 0, 0, tiled=True)
    out_sum = jnp.sum(swapped.astype(F32), axis=0)

    pairs = 2 * count
    factor = jnp.einsum(
        "kel,elr->ekr",
        out_sum.reshape(ranks, 2 * pairs, length),
        in_factor.reshape(2 * pairs, length, rank),
        precision=lax.Precision.HIGHEST,
    ).reshape(pairs, 2, ranks * rank)
    docs = factor[:, 0]
    queries = factor[:, 1]
    doc_squares = jnp.sum(docs * docs, axis=1)
    docs = docs.astype(BF16)
    queries = queries.astype(BF16)

    everyone = lax.all_to_all(
        jnp.broadcast_to(queries[None], (n_fsdp,) + queries.shape), fsdp, 0, 0, tiled=True
    ).reshape(n_fsdp * pairs, -1)
    wide = everyone.astype(F32)
    query_squares = jnp.sum(wide * wide, axis=1)
    scores = lax.dot_general(
        docs, everyone, (((1,), (1,)), ((), ())), preferred_element_type=F32
    )
    total = scores.shape[1]

    def to_destinations(x):
        return x.reshape((2, count) + x.shape[1:]).swapaxes(0, 1).reshape(x.shape)

    payload = jnp.concatenate(
        (
            to_destinations(scores),
            jnp.broadcast_to(query_squares[None], (pairs, total)),
            jnp.broadcast_to(to_destinations(doc_squares)[:, None], (pairs, 128)),
        ),
        axis=1,
    )
    received = lax.all_to_all(payload, dq, 0, 0, tiled=True)
    sums = jnp.sum(received, axis=0)
    entries = 1.0 / (rank * 2 * rank)
    doc_scale = lax.rsqrt(sums[2 * total] * entries + 1e-06)
    query_scale = lax.rsqrt(sums[total : 2 * total] * entries + 1e-06)
    result = sums[:total] * query_scale * (doc_scale / rank)
    return result.reshape(1, 1, total)


def solution(mesh):
    fine = jax.sharding.Mesh(
        mesh.devices.reshape(2, mesh.shape["fsdp"] // 2, mesh.shape["dp"] // 2, 2, 2),
        ("ylo", "z", "x", "core", "yhi"),
    )
    fsdp = ("ylo", "z")
    dp = ("x", "core")
    return jax.shard_map(
        body,
        mesh=fine,
        in_specs=(
            P(fsdp + ("yhi",), None, None),
            P(fsdp + ("yhi",), None, dp),
            P(fsdp + ("yhi",), None, None),
            P(fsdp + ("yhi",), None, dp),
            P(fsdp, dp + ("yhi",)),
            P(fsdp, dp + ("yhi",)),
            P(),
            P(None, dp),
            P(None, dp),
        ),
        out_specs=P(fsdp + ("yhi",), dp, None),
        check_vma=False,
    )
```

```python
import jax
import jax.numpy as jnp
from jax import lax
from jax.sharding import PartitionSpec as P

F32 = jnp.float32
BF16 = jnp.bfloat16

def shift(value, axis, step):
    size = lax.axis_size(axis)
    return lax.ppermute(value, axis, [(i, (i + step) % size) for i in range(size)])


def gathered(weight, piece, cot):
    barrier = lax.optimization_barrier
    n_z = lax.axis_size("z")
    z = lax.axis_index("z")
    full = weight.shape[0]
    half = full // 2

    def up(value):
        return shift(value, "z", 1)

    def down(value):
        return shift(value, "z", -1)

    def across(value):
        return shift(value, "ylo", 1)

    def placed(by_offset):
        result = jnp.zeros((n_z,) + weight.shape, weight.dtype)
        for offset, shard in by_offset:
            result = lax.dynamic_update_slice(result, shard[None], ((z + offset) % n_z, 0, 0))
        return result

    a1, b1, here, w0, cot = barrier(
        (up(weight), down(weight), shift(piece, "yhi", 1), weight, cot)
    )
    partner = lax.all_gather(here, ("x", "core"), axis=0, tiled=True)
    a2, b2, o0 = barrier((up(a1), down(b1), across(w0)))
    a3, b3, oa2, o0, b2 = barrier((up(a2), down(b2), across(a2), o0, b2))
    oa1, ob1, ob2, a4, b4, oa2, cot = barrier(
        (up(o0), down(o0), across(b2), up(a3[:half]), down(b3[half:]), oa2, cot)
    )
    oa3, ob3, other_cot = barrier((up(oa2), down(ob2), shift(cot, "yhi", 1)))
    far = (up(oa3[:half]), down(ob3[half:]))

    this_row = placed(
        ((0, w0), (n_z - 1, a1), (1, b1), (n_z - 2, a2), (2, b2), (n_z - 3, a3), (3, b3))
    )
    far_z = (z + n_z // 2) % n_z
    this_row = lax.dynamic_update_slice(this_row, a4[None], (far_z, 0, 0))
    this_row = lax.dynamic_update_slice(this_row, b4[None], (far_z, half, 0))
    other_row = placed(
        ((0, o0), (n_z - 1, oa1), (1, ob1), (n_z - 2, oa2), (2, ob2), (n_z - 3, oa3), (3, ob3))
    )
    flat = (n_z * full, -1)
    return this_row.reshape(flat), other_row.reshape(flat), far, far_z, other_cot, partner


def projected(pre, cotangent, gate_projection, up_projection):
    cols = pre.shape[1] // 2
    gate = pre[:, :cols]
    up = pre[:, cols:]
    sigma = jax.nn.sigmoid(gate)
    upstream = cotangent.astype(F32)
    gate_grad = (upstream * up * sigma * (1.0 + gate * (1.0 - sigma))).astype(BF16)
    up_grad = (upstream * gate * sigma).astype(BF16)
    dims = (((1,), (1,)), ((), ()))
    return jnp.concatenate(
        (
            lax.dot_general(gate_projection, gate_grad, dims, preferred_element_type=F32),
            lax.dot_general(up_projection, up_grad, dims, preferred_element_type=F32),
        ),
        axis=0,
    )


def body(
    doc_inputs,
    doc_cotangents,
    query_inputs,
    query_cotangents,
    gate_weight,
    up_weight,
    input_projection,
    gate_projection,
    up_projection,
):
    count, length, width = doc_inputs.shape
    half_index = lax.axis_index("yhi")
    row_index = lax.axis_index("ylo")
    dq = ("x", "core", "yhi")
    fsdp = ("ylo", "z")
    n_dq = lax.axis_size(dq)
    n_fsdp = lax.axis_size(fsdp)
    rank = input_projection.shape[0]
    cols = gate_weight.shape[1]

    place = lax.axis_index(("x", "core"))
    piece = jnp.concatenate(
        (
            lax.dynamic_slice_in_dim(doc_inputs, place, 1, 0),
            lax.dynamic_slice_in_dim(query_inputs, place, 1, 0),
        ),
        axis=1,
    )
    own = jnp.concatenate((doc_inputs, query_inputs), axis=1)

    def columns(value, index):
        return lax.dynamic_slice_in_dim(value, index * cols, cols, value.ndim - 1)

    def cotangents(index):
        joined = jnp.concatenate(
            (columns(doc_cotangents, index), columns(query_cotangents, index)), axis=1
        )
        return joined.reshape(-1, cols)

    own_cot = cotangents(half_index)
    weight = jnp.concatenate((gate_weight, up_weight), axis=1)
    this_row, other_row, far, far_z, other_cot, other = gathered(
        weight, piece, cotangents(1 - half_index)
    )
    gate_proj = lax.dynamic_slice_in_dim(gate_projection, half_index * cols, cols, 1)
    up_proj = lax.dynamic_slice_in_dim(up_projection, half_index * cols, cols, 1)

    depth = this_row.shape[0]
    both = []
    for rows in (own, other):
        flat = rows.reshape(-1, width)
        this_flat = lax.dynamic_slice_in_dim(flat, row_index * depth, depth, 1)
        other_flat = lax.dynamic_slice_in_dim(flat, (1 - row_index) * depth, depth, 1)
        pre = jnp.dot(this_flat, this_row, preferred_element_type=F32)
        pre = pre + jnp.dot(other_flat, other_row, preferred_element_type=F32)
        far_flat = lax.dynamic_slice_in_dim(
            other_flat, far_z * weight.shape[0], weight.shape[0], 1
        )
        in_factor = lax.dot_general(
            flat, input_projection, (((1,), (1,)), ((), ())), preferred_element_type=F32
        )
        both.append((pre, far_flat, in_factor))
    both, far = lax.optimization_barrier((both, far))
    far = jnp.concatenate(far, axis=0)
    parts = []
    factors = []
    for (pre, far_flat, in_factor), rows_cot in zip(both, (own_cot, other_cot)):
        pre = pre + jnp.dot(far_flat, far, preferred_element_type=F32)
        parts.append(projected(pre, rows_cot, gate_proj, up_proj))
        factors.append(in_factor)

    first = half_index == 0

    def ordered(pair, axis):
        a = jnp.where(first, pair[0], pair[1])
        b = jnp.where(first, pair[1], pair[0])
        return jnp.concatenate((a, b), axis=axis)

    part = ordered(parts, 1).astype(BF16)
    in_factor = ordered(factors, 0)
    ranks = part.shape[0] // n_dq
    part = part.reshape(n_dq, ranks, -1)
    swapped = lax.all_to_all(part, dq, 0, 0, tiled=True)
    out_sum = jnp.sum(swapped.astype(F32), axis=0)

    pairs = 2 * count
    factor = jnp.einsum(
        "kel,elr->ekr",
        out_sum.reshape(ranks, 2 * pairs, length),
        in_factor.reshape(2 * pairs, length, rank),
        precision=lax.Precision.HIGHEST,
    ).reshape(pairs, 2, ranks * rank)
    docs = factor[:, 0]
    queries = factor[:, 1]
    doc_squares = jnp.sum(docs * docs, axis=1)
    docs = docs.astype(BF16)
    queries = queries.astype(BF16)

    everyone = lax.all_to_all(
        jnp.broadcast_to(queries[None], (n_fsdp,) + queries.shape), fsdp, 0, 0, tiled=True
    ).reshape(n_fsdp * pairs, -1)
    wide = everyone.astype(F32)
    query_squares = jnp.sum(wide * wide, axis=1)
    scores = lax.dot_general(
        docs, everyone, (((1,), (1,)), ((), ())), preferred_element_type=F32
    )
    total = scores.shape[1]

    def to_destinations(x):
        return x.reshape((2, count) + x.shape[1:]).swapaxes(0, 1).reshape(x.shape)

    payload = jnp.concatenate(
        (
            to_destinations(scores),
            jnp.broadcast_to(query_squares[None], (pairs, total)),
            jnp.broadcast_to(to_destinations(doc_squares)[:, None], (pairs, 128)),
        ),
        axis=1,
    )
    received = lax.all_to_all(payload, dq, 0, 0, tiled=True)
    sums = jnp.sum(received, axis=0)
    entries = 1.0 / (rank * 2 * rank)
    doc_scale = lax.rsqrt(sums[2 * total] * entries + 1e-06)
    query_scale = lax.rsqrt(sums[total : 2 * total] * entries + 1e-06)
    result = sums[:total] * query_scale * (doc_scale / rank)
    return result.reshape(1, 1, total)


def solution(mesh):
    fine = jax.sharding.Mesh(
        mesh.devices.reshape(2, mesh.shape["fsdp"] // 2, mesh.shape["dp"] // 2, 2, 2),
        ("ylo", "z", "x", "core", "yhi"),
    )
    fsdp = ("ylo", "z")
    dp = ("x", "core")
    return jax.shard_map(
        body,
        mesh=fine,
        in_specs=(
            P(fsdp + ("yhi",), None, None),
            P(fsdp + ("yhi",), None, dp),
            P(fsdp + ("yhi",), None, None),
            P(fsdp + ("yhi",), None, dp),
            P(fsdp, dp + ("yhi",)),
            P(fsdp, dp + ("yhi",)),
            P(),
            P(None, dp),
            P(None, dp),
        ),
        out_specs=P(fsdp + ("yhi",), dp, None),
        check_vma=False,
    )
```

```python
import jax
import jax.numpy as jnp
from jax import lax
from jax.sharding import PartitionSpec as P

F32 = jnp.float32
BF16 = jnp.bfloat16

def shift(value, axis, step):
    size = lax.axis_size(axis)
    return lax.ppermute(value, axis, [(i, (i + step) % size) for i in range(size)])


def gathered(weight, piece, cot, early):
    barrier = lax.optimization_barrier
    n_z = lax.axis_size("z")
    z = lax.axis_index("z")
    half = weight.shape[0] // 2
    far_z = (z + n_z // 2) % n_z

    def up(value):
        return shift(value, "z", 1)

    def down(value):
        return shift(value, "z", -1)

    def across(value):
        return shift(value, "ylo", 1)

    def placed(by_offset):
        result = jnp.zeros((n_z,) + weight.shape, weight.dtype)
        for offset, shard in by_offset:
            result = lax.dynamic_update_slice(result, shard[None], ((z + offset) % n_z, 0, 0))
        return result.reshape(n_z * weight.shape[0], -1)

    a1, b1, here, w0, cot, early = barrier(
        (up(weight), down(weight), shift(piece, "yhi", 1), weight, cot, early)
    )
    partner = lax.all_gather(here, ("x", "core"), axis=0, tiled=True)
    a2, b2, o0, cot = barrier((up(a1), down(b1), across(w0), cot))
    a3, b3, oa2, o0, b2 = barrier((up(a2), down(b2), across(a2), o0, b2))
    other_cot = shift(cot, "yhi", 1)
    oa1, ob1, ob2, a4, b4, oa2, other_cot = barrier(
        (up(o0), down(o0), across(b2), up(a3[:half]), down(b3[half:]), oa2, other_cot)
    )
    a4 = jnp.concatenate((a4, b4), axis=0)
    last = (
        (across(a4), far_z),
        (up(oa2), (z + n_z - 3) % n_z),
        (down(ob2), (z + 3) % n_z),
    )
    this_row = placed(
        (
            (0, w0),
            (n_z - 1, a1),
            (1, b1),
            (n_z - 2, a2),
            (2, b2),
            (n_z - 3, a3),
            (3, b3),
            (n_z // 2, a4),
        )
    )
    other_row = placed(((0, o0), (n_z - 1, oa1), (1, ob1), (n_z - 2, oa2), (2, ob2)))
    return this_row, other_row, last, other_cot, partner, early


def projected(pre, cotangent, gate_projection, up_projection):
    cols = pre.shape[1] // 2
    gate = pre[:, :cols]
    up = pre[:, cols:]
    sigma = jax.nn.sigmoid(gate)
    upstream = cotangent.astype(F32)
    gate_grad = (upstream * up * sigma * (1.0 + gate * (1.0 - sigma))).astype(BF16)
    up_grad = (upstream * gate * sigma).astype(BF16)
    dims = (((1,), (1,)), ((), ()))
    return jnp.concatenate(
        (
            lax.dot_general(gate_projection, gate_grad, dims, preferred_element_type=F32),
            lax.dot_general(up_projection, up_grad, dims, preferred_element_type=F32),
        ),
        axis=0,
    )


def body(
    doc_inputs,
    doc_cotangents,
    query_inputs,
    query_cotangents,
    gate_weight,
    up_weight,
    input_projection,
    gate_projection,
    up_projection,
):
    count, length, width = doc_inputs.shape
    half_index = lax.axis_index("yhi")
    row_index = lax.axis_index("ylo")
    dq = ("x", "core", "yhi")
    fsdp = ("ylo", "z")
    n_dq = lax.axis_size(dq)
    n_fsdp = lax.axis_size(fsdp)
    rank = input_projection.shape[0]
    cols = gate_weight.shape[1]

    place = lax.axis_index(("x", "core"))
    piece = jnp.concatenate(
        (
            lax.dynamic_slice_in_dim(doc_inputs, place, 1, 0),
            lax.dynamic_slice_in_dim(query_inputs, place, 1, 0),
        ),
        axis=1,
    )
    own = jnp.concatenate((doc_inputs, query_inputs), axis=1)

    def columns(value, index):
        return lax.dynamic_slice_in_dim(value, index * cols, cols, value.ndim - 1)

    def cotangents(index):
        joined = jnp.concatenate(
            (columns(doc_cotangents, index), columns(query_cotangents, index)), axis=1
        )
        return joined.reshape(-1, cols)

    own_cot = cotangents(half_index)
    weight = jnp.concatenate((gate_weight, up_weight), axis=1)
    this_row, other_row, last, other_cot, other, (own, own_cot) = gathered(
        weight, piece, cotangents(1 - half_index), (own, own_cot)
    )
    gate_proj = columns(gate_projection, half_index)
    up_proj = columns(up_projection, half_index)

    depth = this_row.shape[0]
    shard_depth = weight.shape[0]
    pres = []
    factors = []
    chunks = []
    for rows in (own, other):
        flat = rows.reshape(-1, width)
        this_flat = lax.dynamic_slice_in_dim(flat, row_index * depth, depth, 1)
        other_flat = lax.dynamic_slice_in_dim(flat, (1 - row_index) * depth, depth, 1)
        pre = jnp.dot(this_flat, this_row, preferred_element_type=F32)
        pres.append(pre + jnp.dot(other_flat, other_row, preferred_element_type=F32))
        factors.append(
            lax.dot_general(
                flat, input_projection, (((1,), (1,)), ((), ())), preferred_element_type=F32
            )
        )
        chunks.append(
            [
                lax.dynamic_slice_in_dim(other_flat, place * shard_depth, shard_depth, 1)
                for _, place in last
            ]
        )
    shards = [shard for shard, _ in last]
    pres, factors, chunks, shards = lax.optimization_barrier((pres, factors, chunks, shards))
    parts = []
    for pre, pieces, rows_cot in zip(pres, chunks, (own_cot, other_cot)):
        for chunk, shard in zip(pieces, shards):
            pre = pre + jnp.dot(chunk, shard, preferred_element_type=F32)
        parts.append(projected(pre, rows_cot, gate_proj, up_proj))

    first = half_index == 0

    def ordered(pair, axis):
        a = jnp.where(first, pair[0], pair[1])
        b = jnp.where(first, pair[1], pair[0])
        return jnp.concatenate((a, b), axis=axis)

    part = ordered(parts, 1).astype(BF16)
    in_factor = ordered(factors, 0)
    ranks = part.shape[0] // n_dq
    part = part.reshape(n_dq, ranks, -1)
    swapped = lax.all_to_all(part, dq, 0, 0, tiled=True)
    out_sum = jnp.sum(swapped.astype(F32), axis=0)

    pairs = 2 * count
    factor = jnp.einsum(
        "kel,elr->ekr",
        out_sum.reshape(ranks, 2 * pairs, length),
        in_factor.reshape(2 * pairs, length, rank),
        precision=lax.Precision.HIGHEST,
    ).reshape(pairs, 2, ranks * rank)
    docs = factor[:, 0]
    queries = factor[:, 1]
    doc_squares = jnp.sum(docs * docs, axis=1)
    docs = docs.astype(BF16)
    queries = queries.astype(BF16)

    everyone = lax.all_to_all(
        jnp.broadcast_to(queries[None], (n_fsdp,) + queries.shape), fsdp, 0, 0, tiled=True
    ).reshape(n_fsdp * pairs, -1)
    wide = everyone.astype(F32)
    query_squares = jnp.sum(wide * wide, axis=1)
    scores = lax.dot_general(
        docs, everyone, (((1,), (1,)), ((), ())), preferred_element_type=F32
    )
    total = scores.shape[1]

    def to_destinations(x):
        return x.reshape((2, count) + x.shape[1:]).swapaxes(0, 1).reshape(x.shape)

    payload = jnp.concatenate(
        (
            to_destinations(scores),
            jnp.broadcast_to(query_squares[None], (pairs, total)),
            jnp.broadcast_to(to_destinations(doc_squares)[:, None], (pairs, 128)),
        ),
        axis=1,
    )
    received = lax.all_to_all(payload, dq, 0, 0, tiled=True)
    sums = jnp.sum(received, axis=0)
    entries = 1.0 / (rank * 2 * rank)
    doc_scale = lax.rsqrt(sums[2 * total] * entries + 1e-06)
    query_scale = lax.rsqrt(sums[total : 2 * total] * entries + 1e-06)
    result = sums[:total] * query_scale * (doc_scale / rank)
    return result.reshape(1, 1, total)


def solution(mesh):
    fine = jax.sharding.Mesh(
        mesh.devices.reshape(2, mesh.shape["fsdp"] // 2, mesh.shape["dp"] // 2, 2, 2),
        ("ylo", "z", "x", "core", "yhi"),
    )
    fsdp = ("ylo", "z")
    dp = ("x", "core")
    return jax.shard_map(
        body,
        mesh=fine,
        in_specs=(
            P(fsdp + ("yhi",), None, None),
            P(fsdp + ("yhi",), None, dp),
            P(fsdp + ("yhi",), None, None),
            P(fsdp + ("yhi",), None, dp),
            P(fsdp, dp + ("yhi",)),
            P(fsdp, dp + ("yhi",)),
            P(),
            P(None, dp),
            P(None, dp),
        ),
        out_specs=P(fsdp + ("yhi",), dp, None),
        check_vma=False,
    )
```

```python
import jax
import jax.numpy as jnp
from jax import lax
from jax.sharding import PartitionSpec as P

F32 = jnp.float32
BF16 = jnp.bfloat16

def shift(value, axis, step):
    size = lax.axis_size(axis)
    return lax.ppermute(value, axis, [(i, (i + step) % size) for i in range(size)])


def chunked(rows, depth):
    n_z = lax.axis_size("z")
    z = lax.axis_index("z")
    row = lax.axis_index("ylo")
    chunks = {}
    for name, side in (("this", row), ("other", 1 - row)):
        for offset in range(n_z):
            place = side * n_z + (z + offset) % n_z
            chunks[name, offset] = lax.dynamic_slice_in_dim(rows, place * depth, depth, 1)
    return chunks


def preactivations(weight, piece, cot, own):
    barrier = lax.optimization_barrier
    depth = weight.shape[0]
    half = depth // 2
    n_z = lax.axis_size("z")

    def up(value):
        return shift(value, "z", 1)

    def down(value):
        return shift(value, "z", -1)

    def across(value):
        return shift(value, "ylo", 1)

    def add(total, chunks, shards):
        for name, offset, shard in shards:
            term = jnp.dot(chunks[name, offset % n_z], shard, preferred_element_type=F32)
            total = term if total is None else total + term
        return total

    here = shift(piece, "yhi", 1)
    own_chunks = chunked(own, depth)
    a1, b1, here, w0, cot, own_chunks = barrier(
        (up(weight), down(weight), here, weight, cot, own_chunks)
    )
    partner = lax.all_gather(here, ("x", "core"), axis=0, tiled=True)
    own_sum = add(None, own_chunks, (("this", 0, w0), ("this", -1, a1), ("this", 1, b1)))
    o0 = across(w0)
    other_cot = shift(cot, "yhi", 1)
    a2, b2, own_sum = barrier((up(a1), down(b1), own_sum))
    own_sum = add(own_sum, own_chunks, (("this", -2, a2), ("this", 2, b2)))
    a3, b3, oa2, o0, b2, own_sum, other_cot = barrier(
        (up(a2), down(b2), across(a2), o0, b2, own_sum, other_cot)
    )
    other_chunks = chunked(partner.reshape(own.shape), depth)
    first = (("this", 0, w0), ("this", -1, a1), ("this", 1, b1), ("this", -2, a2), ("this", 2, b2))
    other_sum = add(None, other_chunks, first)
    own_sum = add(own_sum, own_chunks, (("this", -3, a3), ("this", 3, b3), ("other", 0, o0)))
    oa1, ob1, ob2, a4, b4, oa2, own_sum, other_sum, other_chunks = barrier(
        (
            up(o0),
            down(o0),
            across(b2),
            up(a3[:half]),
            down(b3[half:]),
            oa2,
            own_sum,
            other_sum,
            other_chunks,
        )
    )
    a4 = jnp.concatenate((a4, b4), axis=0)
    o4 = across(a4)
    oa3 = up(oa2)
    ob3 = down(ob2)
    late = (
        ("this", n_z // 2, a4),
        ("other", -1, oa1),
        ("other", 1, ob1),
        ("other", -2, oa2),
        ("other", 2, ob2),
    )
    own_sum = add(own_sum, own_chunks, late)
    other_sum = add(other_sum, other_chunks, (("this", -3, a3), ("this", 3, b3), ("other", 0, o0)))
    other_sum = add(other_sum, other_chunks, late)
    oa3, ob3, o4, own_sum, other_sum = barrier((oa3, ob3, o4, own_sum, other_sum))
    last = (("other", -3, oa3), ("other", 3, ob3), ("other", n_z // 2, o4))
    own_sum = add(own_sum, own_chunks, last)
    other_sum = add(other_sum, other_chunks, last)
    return own_sum, other_sum, other_cot, partner


def projected(pre, cotangent, gate_projection, up_projection):
    cols = pre.shape[1] // 2
    gate = pre[:, :cols]
    up = pre[:, cols:]
    sigma = jax.nn.sigmoid(gate)
    upstream = cotangent.astype(F32)
    gate_grad = (upstream * up * sigma * (1.0 + gate * (1.0 - sigma))).astype(BF16)
    up_grad = (upstream * gate * sigma).astype(BF16)
    dims = (((1,), (1,)), ((), ()))
    return jnp.concatenate(
        (
            lax.dot_general(gate_projection, gate_grad, dims, preferred_element_type=F32),
            lax.dot_general(up_projection, up_grad, dims, preferred_element_type=F32),
        ),
        axis=0,
    )


def body(
    doc_inputs,
    doc_cotangents,
    query_inputs,
    query_cotangents,
    gate_weight,
    up_weight,
    input_projection,
    gate_projection,
    up_projection,
):
    count, length, width = doc_inputs.shape
    half_index = lax.axis_index("yhi")
    row_index = lax.axis_index("ylo")
    dq = ("x", "core", "yhi")
    fsdp = ("ylo", "z")
    n_dq = lax.axis_size(dq)
    n_fsdp = lax.axis_size(fsdp)
    rank = input_projection.shape[0]
    cols = gate_weight.shape[1]

    place = lax.axis_index(("x", "core"))
    piece = jnp.concatenate(
        (
            lax.dynamic_slice_in_dim(doc_inputs, place, 1, 0),
            lax.dynamic_slice_in_dim(query_inputs, place, 1, 0),
        ),
        axis=1,
    )
    own = jnp.concatenate((doc_inputs, query_inputs), axis=1)

    def columns(value, index):
        return lax.dynamic_slice_in_dim(value, index * cols, cols, value.ndim - 1)

    def cotangents(index):
        joined = jnp.concatenate(
            (columns(doc_cotangents, index), columns(query_cotangents, index)), axis=1
        )
        return joined.reshape(-1, cols)

    own_cot = cotangents(half_index)
    piece, gate_weight, up_weight = lax.optimization_barrier((piece, gate_weight, up_weight))
    weight = jnp.concatenate((gate_weight, up_weight), axis=1)
    own = own.reshape(-1, width)
    own_pre, other_pre, other_cot, other = preactivations(
        weight, piece, cotangents(1 - half_index), own
    )
    gate_proj = columns(gate_projection, half_index)
    up_proj = columns(up_projection, half_index)
    parts = (
        projected(own_pre, own_cot, gate_proj, up_proj),
        projected(other_pre, other_cot, gate_proj, up_proj),
    )
    factors = [
        lax.dot_general(
            rows, input_projection, (((1,), (1,)), ((), ())), preferred_element_type=F32
        )
        for rows in (own, other.reshape(own.shape))
    ]

    first = half_index == 0

    def ordered(pair, axis):
        a = jnp.where(first, pair[0], pair[1])
        b = jnp.where(first, pair[1], pair[0])
        return jnp.concatenate((a, b), axis=axis)

    part = ordered(parts, 1).astype(BF16)
    in_factor = ordered(factors, 0)
    ranks = part.shape[0] // n_dq
    part = part.reshape(n_dq, ranks, -1)
    swapped = lax.all_to_all(part, dq, 0, 0, tiled=True)
    out_sum = jnp.sum(swapped.astype(F32), axis=0)

    pairs = 2 * count
    factor = jnp.einsum(
        "kel,elr->ekr",
        out_sum.reshape(ranks, 2 * pairs, length),
        in_factor.reshape(2 * pairs, length, rank),
        precision=lax.Precision.HIGHEST,
    ).reshape(pairs, 2, ranks * rank)
    docs = factor[:, 0]
    queries = factor[:, 1]
    doc_squares = jnp.sum(docs * docs, axis=1)
    docs = docs.astype(BF16)
    queries = queries.astype(BF16)

    everyone = lax.all_to_all(
        jnp.broadcast_to(queries[None], (n_fsdp,) + queries.shape), fsdp, 0, 0, tiled=True
    ).reshape(n_fsdp * pairs, -1)
    wide = everyone.astype(F32)
    query_squares = jnp.sum(wide * wide, axis=1)
    scores = lax.dot_general(
        docs, everyone, (((1,), (1,)), ((), ())), preferred_element_type=F32
    )
    total = scores.shape[1]

    def to_destinations(x):
        return x.reshape((2, count) + x.shape[1:]).swapaxes(0, 1).reshape(x.shape)

    payload = jnp.concatenate(
        (
            to_destinations(scores),
            jnp.broadcast_to(query_squares[None], (pairs, total)),
            jnp.broadcast_to(to_destinations(doc_squares)[:, None], (pairs, 128)),
        ),
        axis=1,
    )
    received = lax.all_to_all(payload, dq, 0, 0, tiled=True)
    sums = jnp.sum(received, axis=0)
    entries = 1.0 / (rank * 2 * rank)
    doc_scale = lax.rsqrt(sums[2 * total] * entries + 1e-06)
    query_scale = lax.rsqrt(sums[total : 2 * total] * entries + 1e-06)
    result = sums[:total] * query_scale * (doc_scale / rank)
    return result.reshape(1, 1, total)


def solution(mesh):
    fine = jax.sharding.Mesh(
        mesh.devices.reshape(2, mesh.shape["fsdp"] // 2, mesh.shape["dp"] // 2, 2, 2),
        ("ylo", "z", "x", "core", "yhi"),
    )
    fsdp = ("ylo", "z")
    dp = ("x", "core")
    return jax.shard_map(
        body,
        mesh=fine,
        in_specs=(
            P(fsdp + ("yhi",), None, None),
            P(fsdp + ("yhi",), None, dp),
            P(fsdp + ("yhi",), None, None),
            P(fsdp + ("yhi",), None, dp),
            P(fsdp, dp + ("yhi",)),
            P(fsdp, dp + ("yhi",)),
            P(),
            P(None, dp),
            P(None, dp),
        ),
        out_specs=P(fsdp + ("yhi",), dp, None),
        check_vma=False,
    )
```

```python
import jax
import jax.numpy as jnp
from jax import lax
from jax.sharding import PartitionSpec as P

F32 = jnp.float32
BF16 = jnp.bfloat16

def shift(value, axis, step):
    size = lax.axis_size(axis)
    return lax.ppermute(value, axis, [(i, (i + step) % size) for i in range(size)])


def gathered(weight, piece, cot, own, row_index):
    barrier = lax.optimization_barrier
    n_z = lax.axis_size("z")
    z = lax.axis_index("z")
    half = weight.shape[0] // 2
    far_z = (z + n_z // 2) % n_z

    def up(value):
        return shift(value, "z", 1)

    def down(value):
        return shift(value, "z", -1)

    def across(value):
        return shift(value, "ylo", 1)

    def placed(by_offset):
        result = jnp.zeros((n_z,) + weight.shape, weight.dtype)
        for offset, shard in by_offset:
            result = lax.dynamic_update_slice(result, shard[None], ((z + offset) % n_z, 0, 0))
        return result.reshape(n_z * weight.shape[0], -1)

    here = shift(piece, "yhi", 1)
    a1, b1, w0, own, cot = barrier((up(weight), down(weight), weight, own, cot))
    a2, b2, o0, cot = barrier((up(a1), down(b1), across(w0), cot))
    here, _ = barrier((here, a2))
    partner = lax.all_gather(here, ("x", "core"), axis=0, tiled=True)
    other_cot = shift(cot, "yhi", 1)
    a3, b3, oa2, o0, b2 = barrier((up(a2), down(b2), across(a2), o0, b2))
    this_row = placed(
        ((0, w0), (n_z - 1, a1), (1, b1), (n_z - 2, a2), (2, b2), (n_z - 3, a3), (3, b3))
    )
    own_sum = this_product(own, this_row, row_index)
    oa1, ob1, ob2, a4, b4, oa2, own_sum, other_cot = barrier(
        (
            up(o0),
            down(o0),
            across(b2),
            up(a3[:half]),
            down(b3[half:]),
            oa2,
            own_sum,
            other_cot,
        )
    )
    a4 = jnp.concatenate((a4, b4), axis=0)
    last = (
        (across(a4), far_z),
        (up(oa2), (z + n_z - 3) % n_z),
        (down(ob2), (z + 3) % n_z),
    )
    other_row = placed(((0, o0), (n_z - 1, oa1), (1, ob1), (n_z - 2, oa2), (2, ob2)))
    return this_row, own_sum, (a4, far_z), other_row, last, other_cot, partner, own


def this_product(rows, this_row, row_index):
    depth = this_row.shape[0]
    this = lax.dynamic_slice_in_dim(rows, row_index * depth, depth, 1)
    return jnp.dot(this, this_row, preferred_element_type=F32)


def projected(pre, cotangent, gate_projection, up_projection):
    cols = pre.shape[1] // 2
    gate = pre[:, :cols]
    up = pre[:, cols:]
    sigma = jax.nn.sigmoid(gate)
    upstream = cotangent.astype(F32)
    gate_grad = (upstream * up * sigma * (1.0 + gate * (1.0 - sigma))).astype(BF16)
    up_grad = (upstream * gate * sigma).astype(BF16)
    dims = (((1,), (1,)), ((), ()))
    return jnp.concatenate(
        (
            lax.dot_general(gate_projection, gate_grad, dims, preferred_element_type=F32),
            lax.dot_general(up_projection, up_grad, dims, preferred_element_type=F32),
        ),
        axis=0,
    )


def body(
    doc_inputs,
    doc_cotangents,
    query_inputs,
    query_cotangents,
    gate_weight,
    up_weight,
    input_projection,
    gate_projection,
    up_projection,
):
    count, length, width = doc_inputs.shape
    half_index = lax.axis_index("yhi")
    row_index = lax.axis_index("ylo")
    dq = ("x", "core", "yhi")
    fsdp = ("ylo", "z")
    n_dq = lax.axis_size(dq)
    n_fsdp = lax.axis_size(fsdp)
    rank = input_projection.shape[0]
    cols = gate_weight.shape[1]

    place = lax.axis_index(("x", "core"))
    piece = jnp.concatenate(
        (
            lax.dynamic_slice_in_dim(doc_inputs, place, 1, 0),
            lax.dynamic_slice_in_dim(query_inputs, place, 1, 0),
        ),
        axis=1,
    )
    own = jnp.concatenate((doc_inputs, query_inputs), axis=1)

    def columns(value, index):
        return lax.dynamic_slice_in_dim(value, index * cols, cols, value.ndim - 1)

    def cotangents(index):
        return jnp.concatenate(
            (columns(doc_cotangents, index), columns(query_cotangents, index)), axis=0
        )

    weight = jnp.concatenate((gate_weight, up_weight), axis=1)
    own = own.reshape(-1, width)
    this_row, own_sum, far, other_row, last, other_cot, partner, own = gathered(
        weight, piece, cotangents(1 - half_index), own, row_index
    )
    partner = partner.reshape(own.shape)
    gate_proj = columns(gate_projection, half_index)
    up_proj = columns(up_projection, half_index)

    depth = this_row.shape[0]
    shard_depth = weight.shape[0]
    pres = []
    factors = []
    chunks = []
    for rows, pre in ((own, own_sum), (partner, None)):
        other_flat = lax.dynamic_slice_in_dim(rows, (1 - row_index) * depth, depth, 1)

        def chunk(side, place):
            return lax.dynamic_slice_in_dim(
                rows, side * depth + place * shard_depth, shard_depth, 1
            )

        if pre is None:
            pre = this_product(rows, this_row, row_index)
        pre = pre + jnp.dot(other_flat, other_row, preferred_element_type=F32)
        pre = pre + jnp.dot(chunk(row_index, far[1]), far[0], preferred_element_type=F32)
        pres.append(pre)
        factors.append(
            lax.dot_general(
                rows, input_projection, (((1,), (1,)), ((), ())), preferred_element_type=F32
            )
        )
        chunks.append([chunk(1 - row_index, place) for _, place in last])
    shards = [shard for shard, _ in last]
    pres, factors, chunks, shards = lax.optimization_barrier((pres, factors, chunks, shards))
    first = half_index == 0

    def ordered(pair, axis):
        a = jnp.where(first, pair[0], pair[1])
        b = jnp.where(first, pair[1], pair[0])
        return jnp.concatenate((a, b), axis=axis)

    totals = []
    for pre, pieces in zip(pres, chunks):
        for piece_of_rows, shard in zip(pieces, shards):
            pre = pre + jnp.dot(piece_of_rows, shard, preferred_element_type=F32)
        totals.append(pre.reshape(count, 2, length, -1))
    own_cots = (columns(doc_cotangents, half_index), columns(query_cotangents, half_index))
    other_cots = other_cot.reshape((2,) + own_cots[0].shape)

    def sent(kind, totals):
        parts = [
            projected(
                pre[:, kind].reshape(count * length, -1),
                cots[kind].reshape(count * length, -1),
                gate_proj,
                up_proj,
            )
            for pre, cots in zip(totals, (own_cots, other_cots))
        ]
        part = ordered(parts, 1).astype(BF16)
        return part.reshape(n_dq, part.shape[0] // n_dq, -1)

    def scattered(part):
        return lax.all_to_all(part, dq, 0, 0, tiled=True)

    pairs = 2 * count

    def factored(kind, swapped):
        out_sum = jnp.sum(swapped.astype(F32), axis=0)
        in_factor = ordered([f.reshape(count, 2, length, rank)[:, kind] for f in factors], 0)
        return jnp.einsum(
            "kel,elr->ekr",
            out_sum.reshape(-1, pairs, length),
            in_factor,
            precision=lax.Precision.HIGHEST,
        ).reshape(pairs, -1)

    query_sent = sent(1, totals)
    query_sent, totals = lax.optimization_barrier((query_sent, totals))
    query_part = scattered(query_sent)
    doc_part = scattered(sent(0, totals))
    queries = factored(1, query_part).astype(BF16)
    everyone = lax.all_to_all(
        jnp.broadcast_to(queries[None], (n_fsdp,) + queries.shape), fsdp, 0, 0, tiled=True
    ).reshape(n_fsdp * pairs, -1)
    docs = factored(0, doc_part)
    doc_squares = jnp.sum(docs * docs, axis=1)
    docs = docs.astype(BF16)
    wide = everyone.astype(F32)
    query_squares = jnp.sum(wide * wide, axis=1)
    scores = lax.dot_general(
        docs, everyone, (((1,), (1,)), ((), ())), preferred_element_type=F32
    )
    total = scores.shape[1]

    def to_destinations(x):
        return x.reshape((2, count) + x.shape[1:]).swapaxes(0, 1).reshape(x.shape)

    payload = jnp.concatenate(
        (
            to_destinations(scores),
            jnp.broadcast_to(query_squares[None], (pairs, total)),
            jnp.broadcast_to(to_destinations(doc_squares)[:, None], (pairs, 128)),
        ),
        axis=1,
    )
    received = lax.all_to_all(payload, dq, 0, 0, tiled=True)
    sums = jnp.sum(received, axis=0)
    entries = 1.0 / (rank * 2 * rank)
    doc_scale = lax.rsqrt(sums[2 * total] * entries + 1e-06)
    query_scale = lax.rsqrt(sums[total : 2 * total] * entries + 1e-06)
    result = sums[:total] * query_scale * (doc_scale / rank)
    return result.reshape(1, 1, total)


def solution(mesh):
    fine = jax.sharding.Mesh(
        mesh.devices.reshape(2, mesh.shape["fsdp"] // 2, mesh.shape["dp"] // 2, 2, 2),
        ("ylo", "z", "x", "core", "yhi"),
    )
    fsdp = ("ylo", "z")
    dp = ("x", "core")
    return jax.shard_map(
        body,
        mesh=fine,
        in_specs=(
            P(fsdp + ("yhi",), None, None),
            P(fsdp + ("yhi",), None, dp),
            P(fsdp + ("yhi",), None, None),
            P(fsdp + ("yhi",), None, dp),
            P(fsdp, dp + ("yhi",)),
            P(fsdp, dp + ("yhi",)),
            P(),
            P(None, dp),
            P(None, dp),
        ),
        out_specs=P(fsdp + ("yhi",), dp, None),
        check_vma=False,
    )
```

```python
import jax
import jax.numpy as jnp
from jax import lax
from jax.sharding import PartitionSpec as P

F32 = jnp.float32
BF16 = jnp.bfloat16

def shift(value, axis, step):
    size = lax.axis_size(axis)
    return lax.ppermute(value, axis, [(i, (i + step) % size) for i in range(size)])


def gathered(weight, piece, cot, early, this_product):
    barrier = lax.optimization_barrier
    n_z = lax.axis_size("z")
    z = lax.axis_index("z")
    half = weight.shape[0] // 2
    far_z = (z + n_z // 2) % n_z

    def up(value):
        return shift(value, "z", 1)

    def down(value):
        return shift(value, "z", -1)

    def across(value):
        return shift(value, "ylo", 1)

    def placed(by_offset):
        result = jnp.zeros((n_z,) + weight.shape, weight.dtype)
        for offset, shard in by_offset:
            result = lax.dynamic_update_slice(result, shard[None], ((z + offset) % n_z, 0, 0))
        return result.reshape(n_z * weight.shape[0], -1)

    a1, b1, here, w0, cot, early = barrier(
        (up(weight), down(weight), shift(piece, "yhi", 1), weight, cot, early)
    )
    partner = lax.all_gather(here, ("x", "core"), axis=0, tiled=True)
    a2, b2, o0, cot = barrier((up(a1), down(b1), across(w0), cot))
    a3, b3, oa2, o0, b2 = barrier((up(a2), down(b2), across(a2), o0, b2))
    other_cot = shift(cot, "yhi", 1)
    this_row = placed(
        ((0, w0), (n_z - 1, a1), (1, b1), (n_z - 2, a2), (2, b2), (n_z - 3, a3), (3, b3))
    )
    own_sum = this_product(early[0], this_row)
    oa1, ob1, ob2, a4, b4, oa2, other_cot, own_sum = barrier(
        (
            up(o0),
            down(o0),
            across(b2),
            up(a3[:half]),
            down(b3[half:]),
            oa2,
            other_cot,
            own_sum,
        )
    )
    a4 = jnp.concatenate((a4, b4), axis=0)
    last = (
        (across(a4), far_z),
        (up(oa2), (z + n_z - 3) % n_z),
        (down(ob2), (z + 3) % n_z),
    )
    other_row = placed(((0, o0), (n_z - 1, oa1), (1, ob1), (n_z - 2, oa2), (2, ob2)))
    sums = (own_sum, this_product(partner, this_row))
    return sums, (a4, far_z), other_row, last, other_cot, partner, early


def projected(pre, cotangent, gate_projection, up_projection):
    cols = pre.shape[1] // 2
    gate = pre[:, :cols]
    up = pre[:, cols:]
    sigma = jax.nn.sigmoid(gate)
    upstream = cotangent.astype(F32)
    gate_grad = (upstream * up * sigma * (1.0 + gate * (1.0 - sigma))).astype(BF16)
    up_grad = (upstream * gate * sigma).astype(BF16)
    dims = (((1,), (1,)), ((), ()))
    return jnp.concatenate(
        (
            lax.dot_general(gate_projection, gate_grad, dims, preferred_element_type=F32),
            lax.dot_general(up_projection, up_grad, dims, preferred_element_type=F32),
        ),
        axis=0,
    )


def body(
    doc_inputs,
    doc_cotangents,
    query_inputs,
    query_cotangents,
    gate_weight,
    up_weight,
    input_projection,
    gate_projection,
    up_projection,
):
    count, length, width = doc_inputs.shape
    half_index = lax.axis_index("yhi")
    row_index = lax.axis_index("ylo")
    dq = ("x", "core", "yhi")
    fsdp = ("ylo", "z")
    n_dq = lax.axis_size(dq)
    n_fsdp = lax.axis_size(fsdp)
    rank = input_projection.shape[0]
    cols = gate_weight.shape[1]

    place = lax.axis_index(("x", "core"))
    piece = jnp.concatenate(
        (
            lax.dynamic_slice_in_dim(doc_inputs, place, 1, 0),
            lax.dynamic_slice_in_dim(query_inputs, place, 1, 0),
        ),
        axis=1,
    )
    own = jnp.concatenate((doc_inputs, query_inputs), axis=1)

    def columns(value, index):
        return lax.dynamic_slice_in_dim(value, index * cols, cols, value.ndim - 1)

    def cotangents(index):
        joined = jnp.concatenate(
            (columns(doc_cotangents, index), columns(query_cotangents, index)), axis=1
        )
        return joined.reshape(-1, cols)

    own_cot = cotangents(half_index)
    weight = jnp.concatenate((gate_weight, up_weight), axis=1)

    def half_of(rows, side, depth):
        return lax.dynamic_slice_in_dim(rows.reshape(-1, width), side * depth, depth, 1)

    def this_product(rows, this_row):
        flat = half_of(rows, row_index, this_row.shape[0])
        return jnp.dot(flat, this_row, preferred_element_type=F32)

    sums, far, other_row, last, other_cot, other, (own, own_cot) = gathered(
        weight, piece, cotangents(1 - half_index), (own, own_cot), this_product
    )
    gate_proj = columns(gate_projection, half_index)
    up_proj = columns(up_projection, half_index)

    def inner_factor(rows):
        return lax.dot_general(
            rows.reshape(-1, width),
            input_projection,
            (((1,), (1,)), ((), ())),
            preferred_element_type=F32,
        )

    depth = other_row.shape[0]
    shard_depth = weight.shape[0]
    pres = []
    chunks = []
    for rows, pre in zip((own, other), sums):
        flat = rows.reshape(-1, width)

        def chunk(side, place):
            return lax.dynamic_slice_in_dim(
                flat, side * depth + place * shard_depth, shard_depth, 1
            )

        other_flat = half_of(rows, 1 - row_index, depth)
        pre = pre + jnp.dot(other_flat, other_row, preferred_element_type=F32)
        pres.append(pre + jnp.dot(chunk(row_index, far[1]), far[0], preferred_element_type=F32))
        chunks.append([chunk(1 - row_index, place) for _, place in last])
    shards = [shard for shard, _ in last]
    own_factor = inner_factor(own)
    pres, chunks, shards, own_factor, other = lax.optimization_barrier(
        (pres, chunks, shards, own_factor, other)
    )
    factors = (own_factor, inner_factor(other))
    parts = []
    for pre, pieces, rows_cot in zip(pres, chunks, (own_cot, other_cot)):
        for chunk, shard in zip(pieces, shards):
            pre = pre + jnp.dot(chunk, shard, preferred_element_type=F32)
        parts.append(projected(pre, rows_cot, gate_proj, up_proj))

    first = half_index == 0

    def ordered(pair, axis):
        a = jnp.where(first, pair[0], pair[1])
        b = jnp.where(first, pair[1], pair[0])
        return jnp.concatenate((a, b), axis=axis)

    part = ordered(parts, 1).astype(BF16)
    in_factor = ordered(factors, 0)
    ranks = part.shape[0] // n_dq
    part = part.reshape(n_dq, ranks, -1)
    swapped = lax.all_to_all(part, dq, 0, 0, tiled=True)
    out_sum = jnp.sum(swapped.astype(F32), axis=0)

    pairs = 2 * count
    factor = jnp.einsum(
        "kel,elr->ekr",
        out_sum.reshape(ranks, 2 * pairs, length),
        in_factor.reshape(2 * pairs, length, rank),
        precision=lax.Precision.HIGHEST,
    ).reshape(pairs, 2, ranks * rank)
    docs = factor[:, 0]
    queries = factor[:, 1]
    doc_squares = jnp.sum(docs * docs, axis=1)
    docs = docs.astype(BF16)
    queries = queries.astype(BF16)

    everyone = lax.all_to_all(
        jnp.broadcast_to(queries[None], (n_fsdp,) + queries.shape), fsdp, 0, 0, tiled=True
    ).reshape(n_fsdp * pairs, -1)
    wide = everyone.astype(F32)
    query_squares = jnp.sum(wide * wide, axis=1)
    scores = lax.dot_general(
        docs, everyone, (((1,), (1,)), ((), ())), preferred_element_type=F32
    )
    total = scores.shape[1]

    def to_destinations(x):
        return x.reshape((2, count) + x.shape[1:]).swapaxes(0, 1).reshape(x.shape)

    payload = jnp.concatenate(
        (
            to_destinations(scores),
            jnp.broadcast_to(query_squares[None], (pairs, total)),
            jnp.broadcast_to(to_destinations(doc_squares)[:, None], (pairs, 128)),
        ),
        axis=1,
    )
    received = lax.all_to_all(payload, dq, 0, 0, tiled=True)
    sums = jnp.sum(received, axis=0)
    entries = 1.0 / (rank * 2 * rank)
    doc_scale = lax.rsqrt(sums[2 * total] * entries + 1e-06)
    query_scale = lax.rsqrt(sums[total : 2 * total] * entries + 1e-06)
    result = sums[:total] * query_scale * (doc_scale / rank)
    return result.reshape(1, 1, total)


def solution(mesh):
    fine = jax.sharding.Mesh(
        mesh.devices.reshape(2, mesh.shape["fsdp"] // 2, mesh.shape["dp"] // 2, 2, 2),
        ("ylo", "z", "x", "core", "yhi"),
    )
    fsdp = ("ylo", "z")
    dp = ("x", "core")
    return jax.shard_map(
        body,
        mesh=fine,
        in_specs=(
            P(fsdp + ("yhi",), None, None),
            P(fsdp + ("yhi",), None, dp),
            P(fsdp + ("yhi",), None, None),
            P(fsdp + ("yhi",), None, dp),
            P(fsdp, dp + ("yhi",)),
            P(fsdp, dp + ("yhi",)),
            P(),
            P(None, dp),
            P(None, dp),
        ),
        out_specs=P(fsdp + ("yhi",), dp, None),
        check_vma=False,
    )
```

```python
import jax
import jax.numpy as jnp
from jax import lax
from jax.experimental import pallas as pl
from jax.experimental.pallas import tpu as pltpu
from jax.sharding import PartitionSpec as P

F32 = jnp.float32
BF16 = jnp.bfloat16

def shift(value, axis, step):
    size = lax.axis_size(axis)
    return lax.ppermute(value, axis, [(i, (i + step) % size) for i in range(size)])


def gathered(weight, piece, cot, early, this_product):
    barrier = lax.optimization_barrier
    n_z = lax.axis_size("z")
    z = lax.axis_index("z")
    half = weight.shape[0] // 2
    far_z = (z + n_z // 2) % n_z

    def up(value):
        return shift(value, "z", 1)

    def down(value):
        return shift(value, "z", -1)

    def across(value):
        return shift(value, "ylo", 1)

    def placed(by_offset):
        result = jnp.zeros((n_z,) + weight.shape, weight.dtype)
        for offset, shard in by_offset:
            result = lax.dynamic_update_slice(result, shard[None], ((z + offset) % n_z, 0, 0))
        return result.reshape(n_z * weight.shape[0], -1)

    a1, b1, here, w0, cot, early = barrier(
        (up(weight), down(weight), shift(piece, "yhi", 1), weight, cot, early)
    )
    partner = lax.all_gather(here, ("x", "core"), axis=0, tiled=True)
    a2, b2, o0, cot = barrier((up(a1), down(b1), across(w0), cot))
    a3, b3, oa2, o0, b2 = barrier((up(a2), down(b2), across(a2), o0, b2))
    other_cot = shift(cot, "yhi", 1)
    this_row = placed(
        ((0, w0), (n_z - 1, a1), (1, b1), (n_z - 2, a2), (2, b2), (n_z - 3, a3), (3, b3))
    )
    own_sum = this_product(early[0], this_row)
    oa1, ob1, ob2, a4, b4, oa2, other_cot, own_sum = barrier(
        (
            up(o0),
            down(o0),
            across(b2),
            up(a3[:half]),
            down(b3[half:]),
            oa2,
            other_cot,
            own_sum,
        )
    )
    a4 = jnp.concatenate((a4, b4), axis=0)
    last = (
        (across(a4), far_z),
        (up(oa2), (z + n_z - 3) % n_z),
        (down(ob2), (z + 3) % n_z),
    )
    other_row = placed(((0, o0), (n_z - 1, oa1), (1, ob1), (n_z - 2, oa2), (2, ob2)))
    return this_row, own_sum, (a4, far_z), other_row, last, other_cot, partner, early


VMEM_LIMIT = 28 * 2**20
ROWS = 256
WHOLE = pl.BlockSpec(memory_space=pltpu.VMEM)


def halves_kernel(side_ref, this_x, other_x, this_row, other_row, out):
    del side_ref
    out[...] = jnp.dot(
        this_x[...], this_row[...], preferred_element_type=F32
    ) + jnp.dot(other_x[...], other_row[...], preferred_element_type=F32)


def halves_product(rows, this_row, other_row, row_index):
    count, width = rows.shape
    depth, cols = this_row.shape
    return pl.pallas_call(
        halves_kernel,
        out_shape=jax.ShapeDtypeStruct((count, cols), F32),
        grid_spec=pltpu.PrefetchScalarGridSpec(
            num_scalar_prefetch=1,
            grid=(count // ROWS,),
            in_specs=[
                pl.BlockSpec((ROWS, depth), lambda i, side: (i, side[0])),
                pl.BlockSpec((ROWS, depth), lambda i, side: (i, 1 - side[0])),
                WHOLE,
                WHOLE,
            ],
            out_specs=pl.BlockSpec((ROWS, cols), lambda i, side: (i, 0)),
        ),
        compiler_params=pltpu.CompilerParams(vmem_limit_bytes=VMEM_LIMIT),
        cost_estimate=pl.CostEstimate(
            flops=2 * count * width * cols,
            bytes_accessed=2 * count * width + 4 * count * cols,
            transcendentals=0,
        ),
        name="halves_product",
    )(row_index.astype(jnp.int32).reshape(1), rows, rows, this_row, other_row)


def finish_kernel(n, *refs):
    sums, cot, projection = refs[0], refs[1], refs[2]
    chunks, shards, out = refs[3 : 3 + n], refs[3 + n : 3 + 2 * n], refs[3 + 2 * n]
    total = sums[...]
    for chunk, shard in zip(chunks, shards):
        total += jnp.dot(chunk[...], shard[...], preferred_element_type=F32)
    half = total.shape[1] // 2
    turned = pltpu.roll(total, half, 1)
    low = lax.broadcasted_iota(jnp.int32, total.shape, 1) < half
    gate = jnp.where(low, total, turned)
    sigma = jax.nn.sigmoid(gate)
    slope = jnp.where(low, turned * (1.0 + gate * (1.0 - sigma)), gate)
    grad = (cot[...].astype(F32) * sigma * slope).astype(BF16)
    out[...] = lax.dot_general(
        projection[...], grad, (((1,), (1,)), ((), ())), preferred_element_type=F32
    ).astype(BF16)


def finished(sums, cot, projection, chunks, shards):
    count, cols = sums.shape
    depth = shards[0].shape[0]
    out_rows = projection.shape[0]
    n = len(shards)
    return pl.pallas_call(
        lambda *refs: finish_kernel(n, *refs),
        out_shape=jax.ShapeDtypeStruct((out_rows, count), BF16),
        grid=(count // ROWS,),
        in_specs=[
            pl.BlockSpec((ROWS, cols), lambda i: (i, 0)),
            pl.BlockSpec((ROWS, cols), lambda i: (i, 0)),
            WHOLE,
        ]
        + [pl.BlockSpec((ROWS, depth), lambda i: (i, 0))] * n
        + [WHOLE] * n,
        out_specs=pl.BlockSpec((out_rows, ROWS), lambda i: (0, i)),
        compiler_params=pltpu.CompilerParams(vmem_limit_bytes=VMEM_LIMIT),
        cost_estimate=pl.CostEstimate(
            flops=2 * count * cols * (n * depth + out_rows),
            bytes_accessed=6 * count * cols + 2 * n * depth * (count + cols),
            transcendentals=count * cols,
        ),
        name="finished",
    )(sums, cot, projection, *chunks, *shards)


def body(
    doc_inputs,
    doc_cotangents,
    query_inputs,
    query_cotangents,
    gate_weight,
    up_weight,
    input_projection,
    gate_projection,
    up_projection,
):
    count, length, width = doc_inputs.shape
    half_index = lax.axis_index("yhi")
    row_index = lax.axis_index("ylo")
    dq = ("x", "core", "yhi")
    fsdp = ("ylo", "z")
    n_dq = lax.axis_size(dq)
    n_fsdp = lax.axis_size(fsdp)
    rank = input_projection.shape[0]
    cols = gate_weight.shape[1]

    place = lax.axis_index(("x", "core"))
    piece = jnp.concatenate(
        (
            lax.dynamic_slice_in_dim(doc_inputs, place, 1, 0),
            lax.dynamic_slice_in_dim(query_inputs, place, 1, 0),
        ),
        axis=1,
    )
    own = jnp.concatenate((doc_inputs, query_inputs), axis=1)

    def columns(value, index):
        return lax.dynamic_slice_in_dim(value, index * cols, cols, value.ndim - 1)

    def cotangents(index):
        joined = jnp.concatenate(
            (columns(doc_cotangents, index), columns(query_cotangents, index)), axis=1
        )
        return joined.reshape(-1, cols)

    own_cot = cotangents(half_index)
    weight = jnp.concatenate((gate_weight, up_weight), axis=1)

    def half_of(rows, side, depth):
        return lax.dynamic_slice_in_dim(rows.reshape(-1, width), side * depth, depth, 1)

    def this_product(rows, this_row):
        flat = half_of(rows, row_index, this_row.shape[0])
        return jnp.dot(flat, this_row, preferred_element_type=F32)

    this_row, own_sum, far, other_row, last, other_cot, other, (own, own_cot) = gathered(
        weight, piece, cotangents(1 - half_index), (own, own_cot), this_product
    )
    gate_proj = columns(gate_projection, half_index)
    up_proj = columns(up_projection, half_index)
    projection = jnp.concatenate(
        (
            jnp.pad(gate_proj, ((0, 0), (0, cols))),
            jnp.pad(up_proj, ((0, 0), (cols, 0))),
        ),
        axis=0,
    )

    def inner_factor(rows):
        return lax.dot_general(
            rows.reshape(-1, width),
            input_projection,
            (((1,), (1,)), ((), ())),
            preferred_element_type=F32,
        )

    depth = other_row.shape[0]
    shard_depth = weight.shape[0]
    chunks = []
    for rows in (own, other):
        flat = rows.reshape(-1, width)

        def chunk(side, place):
            return lax.dynamic_slice_in_dim(
                flat, side * depth + place * shard_depth, shard_depth, 1
            )

        chunks.append(
            [chunk(row_index, far[1])] + [chunk(1 - row_index, place) for _, place in last]
        )
    own_sum = own_sum + jnp.dot(
        half_of(own, 1 - row_index, depth), other_row, preferred_element_type=F32
    )
    other_sum = halves_product(other.reshape(-1, width), this_row, other_row, row_index)
    twice = [jnp.concatenate((cot, cot), axis=1) for cot in (own_cot, other_cot)]
    own_factor = inner_factor(own)
    shards = [far[0]] + [shard for shard, _ in last]
    own_sum, other_sum, twice, projection, chunks, shards, own_factor, other = (
        lax.optimization_barrier(
            (own_sum, other_sum, twice, projection, chunks, shards, own_factor, other)
        )
    )
    factors = (own_factor, inner_factor(other))
    parts = [
        finished(sums, cot, projection, pieces, shards)
        for sums, cot, pieces in zip((own_sum, other_sum), twice, chunks)
    ]

    first = half_index == 0

    def ordered(pair, axis):
        a = jnp.where(first, pair[0], pair[1])
        b = jnp.where(first, pair[1], pair[0])
        return jnp.concatenate((a, b), axis=axis)

    part = ordered(parts, 1)
    in_factor = ordered(factors, 0)
    ranks = part.shape[0] // n_dq
    part = part.reshape(n_dq, ranks, -1)
    swapped = lax.all_to_all(part, dq, 0, 0, tiled=True)
    out_sum = jnp.sum(swapped.astype(F32), axis=0)

    pairs = 2 * count
    factor = jnp.einsum(
        "kel,elr->ekr",
        out_sum.reshape(ranks, 2 * pairs, length),
        in_factor.reshape(2 * pairs, length, rank),
        precision=lax.Precision.HIGHEST,
    ).reshape(pairs, 2, ranks * rank)
    docs = factor[:, 0]
    queries = factor[:, 1]
    doc_squares = jnp.sum(docs * docs, axis=1)
    docs = docs.astype(BF16)
    queries = queries.astype(BF16)

    everyone = lax.all_to_all(
        jnp.broadcast_to(queries[None], (n_fsdp,) + queries.shape), fsdp, 0, 0, tiled=True
    ).reshape(n_fsdp * pairs, -1)
    wide = everyone.astype(F32)
    query_squares = jnp.sum(wide * wide, axis=1)
    scores = lax.dot_general(
        docs, everyone, (((1,), (1,)), ((), ())), preferred_element_type=F32
    )
    total = scores.shape[1]

    def to_destinations(x):
        return x.reshape((2, count) + x.shape[1:]).swapaxes(0, 1).reshape(x.shape)

    payload = jnp.concatenate(
        (
            to_destinations(scores),
            jnp.broadcast_to(query_squares[None], (pairs, total)),
            jnp.broadcast_to(to_destinations(doc_squares)[:, None], (pairs, 128)),
        ),
        axis=1,
    )
    received = lax.all_to_all(payload, dq, 0, 0, tiled=True)
    sums = jnp.sum(received, axis=0)
    entries = 1.0 / (rank * 2 * rank)
    doc_scale = lax.rsqrt(sums[2 * total] * entries + 1e-06)
    query_scale = lax.rsqrt(sums[total : 2 * total] * entries + 1e-06)
    result = sums[:total] * query_scale * (doc_scale / rank)
    return result.reshape(1, 1, total)


def solution(mesh):
    fine = jax.sharding.Mesh(
        mesh.devices.reshape(2, mesh.shape["fsdp"] // 2, mesh.shape["dp"] // 2, 2, 2),
        ("ylo", "z", "x", "core", "yhi"),
    )
    fsdp = ("ylo", "z")
    dp = ("x", "core")
    return jax.shard_map(
        body,
        mesh=fine,
        in_specs=(
            P(fsdp + ("yhi",), None, None),
            P(fsdp + ("yhi",), None, dp),
            P(fsdp + ("yhi",), None, None),
            P(fsdp + ("yhi",), None, dp),
            P(fsdp, dp + ("yhi",)),
            P(fsdp, dp + ("yhi",)),
            P(),
            P(None, dp),
            P(None, dp),
        ),
        out_specs=P(fsdp + ("yhi",), dp, None),
        check_vma=False,
    )
```

```python
import jax
import jax.numpy as jnp
from jax import lax
from jax.sharding import PartitionSpec as P

F32 = jnp.float32
BF16 = jnp.bfloat16

def shift(value, axis, step):
    size = lax.axis_size(axis)
    return lax.ppermute(value, axis, [(i, (i + step) % size) for i in range(size)])


def gathered(weight, piece, cot, early, start):
    barrier = lax.optimization_barrier
    n_z = lax.axis_size("z")
    z = lax.axis_index("z")
    half = weight.shape[0] // 2
    this = lax.axis_index("ylo") * n_z
    other = n_z - this

    def up(value):
        return shift(value, "z", 1)

    def down(value):
        return shift(value, "z", -1)

    def across(value):
        return shift(value, "ylo", 1)

    a1, b1, here, w0, cot, early = barrier(
        (up(weight), down(weight), shift(piece, "yhi", 1), weight, cot, early)
    )
    partner = lax.all_gather(here, ("x", "core"), axis=0, tiled=True)
    a2, b2, o0, cot = barrier((up(a1), down(b1), across(w0), cot))
    a3, b3, oa2, o0, b2 = barrier((up(a2), down(b2), across(a2), o0, b2))
    other_cot = shift(cot, "yhi", 1)
    oa1, ob1, ob2, a4, b4, oa2, other_cot = barrier(
        (up(o0), down(o0), across(b2), up(a3[:half]), down(b3[half:]), oa2, other_cot)
    )
    a4 = jnp.concatenate((a4, b4), axis=0)
    last = (
        (across(a4), other + (z + n_z // 2) % n_z),
        (up(oa2), other + (z + n_z - 3) % n_z),
        (down(ob2), other + (z + 3) % n_z),
    )
    def placed(joined, shards):
        for side, offset, shard in shards:
            at = side + (z + offset) % n_z
            joined = lax.dynamic_update_slice(joined, shard[None], (at, 0, 0))
        return joined

    joined = placed(
        start.reshape(2 * n_z, weight.shape[0], -1),
        (
            (this, 0, w0),
            (this, n_z - 1, a1),
            (this, 1, b1),
            (this, n_z - 2, a2),
            (this, 2, b2),
            (other, 0, o0),
            (this, n_z - 3, a3),
            (this, 3, b3),
            (other, n_z - 2, oa2),
        ),
    )
    joined, partner, early = barrier((joined, partner, early))
    joined = placed(
        joined,
        (
            (this, n_z // 2, a4),
            (other, n_z - 1, oa1),
            (other, 1, ob1),
            (other, 2, ob2),
        ),
    )
    return joined.reshape(start.shape), last, other_cot, partner, early


def projected(pre, cotangent, gate_projection, up_projection):
    cols = pre.shape[1] // 2
    gate = pre[:, :cols]
    up = pre[:, cols:]
    sigma = jax.nn.sigmoid(gate)
    upstream = cotangent.astype(F32)
    gate_grad = (upstream * up * sigma * (1.0 + gate * (1.0 - sigma))).astype(BF16)
    up_grad = (upstream * gate * sigma).astype(BF16)
    dims = (((1,), (1,)), ((), ()))
    return jnp.concatenate(
        (
            lax.dot_general(gate_projection, gate_grad, dims, preferred_element_type=F32),
            lax.dot_general(up_projection, up_grad, dims, preferred_element_type=F32),
        ),
        axis=0,
    )


def body(
    doc_inputs,
    doc_cotangents,
    query_inputs,
    query_cotangents,
    gate_weight,
    up_weight,
    input_projection,
    gate_projection,
    up_projection,
):
    count, length, width = doc_inputs.shape
    half_index = lax.axis_index("yhi")
    row_index = lax.axis_index("ylo")
    dq = ("x", "core", "yhi")
    fsdp = ("ylo", "z")
    n_dq = lax.axis_size(dq)
    n_fsdp = lax.axis_size(fsdp)
    rank = input_projection.shape[0]
    cols = gate_weight.shape[1]

    place = lax.axis_index(("x", "core"))
    piece = jnp.concatenate(
        (
            lax.dynamic_slice_in_dim(doc_inputs, place, 1, 0),
            lax.dynamic_slice_in_dim(query_inputs, place, 1, 0),
        ),
        axis=1,
    )
    own = jnp.concatenate((doc_inputs, query_inputs), axis=1)

    def columns(value, index):
        return lax.dynamic_slice_in_dim(value, index * cols, cols, value.ndim - 1)

    def cotangents(index):
        joined = jnp.concatenate(
            (columns(doc_cotangents, index), columns(query_cotangents, index)), axis=1
        )
        return joined.reshape(-1, cols)

    own_cot = cotangents(half_index)
    piece, gate_weight, up_weight = lax.optimization_barrier((piece, gate_weight, up_weight))
    weight = jnp.concatenate((gate_weight, up_weight), axis=1)
    wide = weight.shape[1]
    start = jnp.pad(input_projection.T, ((0, 0), (wide, 0)))
    joined, last, other_cot, other, (own, own_cot) = gathered(
        weight, piece, cotangents(1 - half_index), (own, own_cot), start
    )
    gate_proj = columns(gate_projection, half_index)
    up_proj = columns(up_projection, half_index)

    depth = weight.shape[0]
    products = []
    chunks = []
    for rows in (own, other):
        flat = rows.reshape(-1, width)
        products.append(jnp.dot(flat, joined, preferred_element_type=F32))
        chunks.append([lax.dynamic_slice_in_dim(flat, at * depth, depth, 1) for _, at in last])
    shards = [shard for shard, _ in last]
    products, chunks, shards = lax.optimization_barrier((products, chunks, shards))
    parts = []
    factors = [product[:, wide:] for product in products]
    for product, pieces, rows_cot in zip(products, chunks, (own_cot, other_cot)):
        pre = product[:, :wide]
        for chunk, shard in zip(pieces, shards):
            pre = pre + jnp.dot(chunk, shard, preferred_element_type=F32)
        parts.append(projected(pre, rows_cot, gate_proj, up_proj))

    first = half_index == 0

    def ordered(pair, axis):
        a = jnp.where(first, pair[0], pair[1])
        b = jnp.where(first, pair[1], pair[0])
        return jnp.concatenate((a, b), axis=axis)

    part = ordered(parts, 1).astype(BF16)
    in_factor = ordered(factors, 0)
    ranks = part.shape[0] // n_dq
    part = part.reshape(n_dq, ranks, -1)
    swapped = lax.all_to_all(part, dq, 0, 0, tiled=True)
    out_sum = jnp.sum(swapped.astype(F32), axis=0)

    pairs = 2 * count
    factor = jnp.einsum(
        "kel,elr->ekr",
        out_sum.reshape(ranks, 2 * pairs, length),
        in_factor.reshape(2 * pairs, length, rank),
        precision=lax.Precision.HIGHEST,
    ).reshape(pairs, 2, ranks * rank)
    docs = factor[:, 0]
    queries = factor[:, 1]
    doc_squares = jnp.sum(docs * docs, axis=1)
    docs = docs.astype(BF16)
    queries = queries.astype(BF16)

    everyone = lax.all_to_all(
        jnp.broadcast_to(queries[None], (n_fsdp,) + queries.shape), fsdp, 0, 0, tiled=True
    ).reshape(n_fsdp * pairs, -1)
    wide = everyone.astype(F32)
    query_squares = jnp.sum(wide * wide, axis=1)
    scores = lax.dot_general(
        docs, everyone, (((1,), (1,)), ((), ())), preferred_element_type=F32
    )
    total = scores.shape[1]

    def to_destinations(x):
        return x.reshape((2, count) + x.shape[1:]).swapaxes(0, 1).reshape(x.shape)

    payload = jnp.concatenate(
        (
            to_destinations(scores),
            jnp.broadcast_to(query_squares[None], (pairs, total)),
            jnp.broadcast_to(to_destinations(doc_squares)[:, None], (pairs, 128)),
        ),
        axis=1,
    )
    received = lax.all_to_all(payload, dq, 0, 0, tiled=True)
    sums = jnp.sum(received, axis=0)
    entries = 1.0 / (rank * 2 * rank)
    doc_scale = lax.rsqrt(sums[2 * total] * entries + 1e-06)
    query_scale = lax.rsqrt(sums[total : 2 * total] * entries + 1e-06)
    result = sums[:total] * query_scale * (doc_scale / rank)
    return result.reshape(1, 1, total)


def solution(mesh):
    fine = jax.sharding.Mesh(
        mesh.devices.reshape(2, mesh.shape["fsdp"] // 2, mesh.shape["dp"] // 2, 2, 2),
        ("ylo", "z", "x", "core", "yhi"),
    )
    fsdp = ("ylo", "z")
    dp = ("x", "core")
    return jax.shard_map(
        body,
        mesh=fine,
        in_specs=(
            P(fsdp + ("yhi",), None, None),
            P(fsdp + ("yhi",), None, dp),
            P(fsdp + ("yhi",), None, None),
            P(fsdp + ("yhi",), None, dp),
            P(fsdp, dp + ("yhi",)),
            P(fsdp, dp + ("yhi",)),
            P(),
            P(None, dp),
            P(None, dp),
        ),
        out_specs=P(fsdp + ("yhi",), dp, None),
        check_vma=False,
    )
```

```python
import jax
import jax.numpy as jnp
from jax import lax
from jax.sharding import PartitionSpec as P

F32 = jnp.float32
BF16 = jnp.bfloat16

def shift(value, axis, step):
    size = lax.axis_size(axis)
    return lax.ppermute(value, axis, [(i, (i + step) % size) for i in range(size)])


def gathered(weight, piece, cot, early, this_product):
    barrier = lax.optimization_barrier
    n_z = lax.axis_size("z")
    z = lax.axis_index("z")
    half = weight.shape[0] // 2
    far_z = (z + n_z // 2) % n_z

    def up(value):
        return shift(value, "z", 1)

    def down(value):
        return shift(value, "z", -1)

    def across(value):
        return shift(value, "ylo", 1)

    def placed(joined, *shards):
        for offset, shard in shards:
            at = (z + offset) % n_z
            joined = lax.dynamic_update_slice(joined, shard[None], (at, 0, 0))
        return joined

    a1, b1, o0, w0, cot, piece, early = barrier(
        (up(weight), down(weight), across(weight), weight, cot, piece, early)
    )
    empty = jnp.zeros((n_z,) + weight.shape, weight.dtype)
    this_row = placed(empty, (0, w0), (n_z - 1, a1), (1, b1))
    other_row = placed(empty, (0, o0))
    a2, b2, here, cot, this_row, other_row = barrier(
        (up(a1), down(b1), shift(piece, "yhi", 1), cot, this_row, other_row)
    )
    partner = lax.all_gather(here, ("x", "core"), axis=0, tiled=True)
    other_cot = shift(cot, "yhi", 1)
    this_row = placed(this_row, (n_z - 2, a2), (2, b2))
    a3, b3, oa2, b2, o0, this_row = barrier((up(a2), down(b2), across(a2), b2, o0, this_row))
    this_row = placed(this_row, (n_z - 3, a3), (3, b3))
    this_row = this_row.reshape(n_z * weight.shape[0], -1)
    own_sum = this_product(early[0], this_row)
    other_row = placed(other_row, (n_z - 2, oa2))
    oa1, ob1, ob2, a4, b4, oa2, other_cot, own_sum, other_row = barrier(
        (
            up(o0),
            down(o0),
            across(b2),
            up(a3[:half]),
            down(b3[half:]),
            oa2,
            other_cot,
            own_sum,
            other_row,
        )
    )
    a4 = jnp.concatenate((a4, b4), axis=0)
    last = (
        (across(a4), far_z),
        (up(oa2), (z + n_z - 3) % n_z),
        (down(ob2), (z + 3) % n_z),
    )
    other_row = placed(other_row, (n_z - 1, oa1), (1, ob1), (2, ob2))
    other_row = other_row.reshape(this_row.shape)
    own_sum, other_row, partner = barrier((own_sum, other_row, partner))
    return this_row, own_sum, (a4, far_z), other_row, last, other_cot, partner, early


def projected(pre, cotangent, gate_projection, up_projection):
    cols = pre.shape[1] // 2
    gate = pre[:, :cols]
    up = pre[:, cols:]
    sigma = jax.nn.sigmoid(gate)
    upstream = cotangent.astype(F32)
    gate_grad = (upstream * up * sigma * (1.0 + gate * (1.0 - sigma))).astype(BF16)
    up_grad = (upstream * gate * sigma).astype(BF16)
    dims = (((1,), (1,)), ((), ()))
    return jnp.concatenate(
        (
            lax.dot_general(gate_projection, gate_grad, dims, preferred_element_type=F32),
            lax.dot_general(up_projection, up_grad, dims, preferred_element_type=F32),
        ),
        axis=0,
    )


def body(
    doc_inputs,
    doc_cotangents,
    query_inputs,
    query_cotangents,
    gate_weight,
    up_weight,
    input_projection,
    gate_projection,
    up_projection,
):
    count, length, width = doc_inputs.shape
    half_index = lax.axis_index("yhi")
    row_index = lax.axis_index("ylo")
    dq = ("x", "core", "yhi")
    fsdp = ("ylo", "z")
    n_dq = lax.axis_size(dq)
    n_fsdp = lax.axis_size(fsdp)
    rank = input_projection.shape[0]
    cols = gate_weight.shape[1]

    place = lax.axis_index(("x", "core"))
    piece = jnp.concatenate(
        (
            lax.dynamic_slice_in_dim(doc_inputs, place, 1, 0),
            lax.dynamic_slice_in_dim(query_inputs, place, 1, 0),
        ),
        axis=1,
    )
    own = jnp.concatenate((doc_inputs, query_inputs), axis=1)

    def columns(value, index):
        return lax.dynamic_slice_in_dim(value, index * cols, cols, value.ndim - 1)

    def cotangents(index):
        joined = jnp.concatenate(
            (columns(doc_cotangents, index), columns(query_cotangents, index)), axis=1
        )
        return joined.reshape(-1, cols)

    own_cot = cotangents(half_index)
    weight = jnp.concatenate((gate_weight, up_weight), axis=1)

    def half_of(rows, side, depth):
        return lax.dynamic_slice_in_dim(rows.reshape(-1, width), side * depth, depth, 1)

    def this_product(rows, this_row):
        flat = half_of(rows, row_index, this_row.shape[0])
        return jnp.dot(flat, this_row, preferred_element_type=F32)

    this_row, own_sum, far, other_row, last, other_cot, other, (own, own_cot) = gathered(
        weight, piece, cotangents(1 - half_index), (own, own_cot), this_product
    )
    gate_proj = columns(gate_projection, half_index)
    up_proj = columns(up_projection, half_index)

    def inner_factor(rows):
        return lax.dot_general(
            rows.reshape(-1, width),
            input_projection,
            (((1,), (1,)), ((), ())),
            preferred_element_type=F32,
        )

    depth = other_row.shape[0]
    shard_depth = weight.shape[0]

    def chunk(rows, side, place):
        return lax.dynamic_slice_in_dim(
            rows.reshape(-1, width), side * depth + place * shard_depth, shard_depth, 1
        )

    def rest(rows, pre):
        pre = pre + jnp.dot(
            half_of(rows, 1 - row_index, depth), other_row, preferred_element_type=F32
        )
        return pre + jnp.dot(
            chunk(rows, row_index, far[1]), far[0], preferred_element_type=F32
        )

    def last_chunks(rows):
        return [chunk(rows, 1 - row_index, place) for _, place in last]

    own_done = (rest(own, own_sum), last_chunks(own), inner_factor(own))
    own_done, other = lax.optimization_barrier((own_done, other))
    other_done = (
        rest(other, this_product(other, this_row)),
        last_chunks(other),
        inner_factor(other),
    )
    shards = [shard for shard, _ in last]
    own_done, other_done, shards = lax.optimization_barrier((own_done, other_done, shards))
    pres, chunks, factors = zip(own_done, other_done)
    parts = []
    for pre, pieces, rows_cot in zip(pres, chunks, (own_cot, other_cot)):
        for chunk, shard in zip(pieces, shards):
            pre = pre + jnp.dot(chunk, shard, preferred_element_type=F32)
        parts.append(projected(pre, rows_cot, gate_proj, up_proj))

    first = half_index == 0

    def ordered(pair, axis):
        a = jnp.where(first, pair[0], pair[1])
        b = jnp.where(first, pair[1], pair[0])
        return jnp.concatenate((a, b), axis=axis)

    part = ordered(parts, 1).astype(BF16)
    in_factor = ordered(factors, 0)
    ranks = part.shape[0] // n_dq
    part = part.reshape(n_dq, ranks, -1)
    swapped = lax.all_to_all(part, dq, 0, 0, tiled=True)
    out_sum = jnp.sum(swapped.astype(F32), axis=0)

    pairs = 2 * count
    factor = jnp.einsum(
        "kel,elr->ekr",
        out_sum.reshape(ranks, 2 * pairs, length),
        in_factor.reshape(2 * pairs, length, rank),
        precision=lax.Precision.HIGHEST,
    ).reshape(pairs, 2, ranks * rank)
    docs = factor[:, 0]
    queries = factor[:, 1]
    doc_squares = jnp.sum(docs * docs, axis=1)
    docs = docs.astype(BF16)
    queries = queries.astype(BF16)

    everyone = lax.all_to_all(
        jnp.broadcast_to(queries[None], (n_fsdp,) + queries.shape), fsdp, 0, 0, tiled=True
    ).reshape(n_fsdp * pairs, -1)
    wide = everyone.astype(F32)
    query_squares = jnp.sum(wide * wide, axis=1)
    scores = lax.dot_general(
        docs, everyone, (((1,), (1,)), ((), ())), preferred_element_type=F32
    )
    total = scores.shape[1]

    def to_destinations(x):
        return x.reshape((2, count) + x.shape[1:]).swapaxes(0, 1).reshape(x.shape)

    payload = jnp.concatenate(
        (
            to_destinations(scores),
            jnp.broadcast_to(query_squares[None], (pairs, total)),
            jnp.broadcast_to(to_destinations(doc_squares)[:, None], (pairs, 128)),
        ),
        axis=1,
    )
    received = lax.all_to_all(payload, dq, 0, 0, tiled=True)
    sums = jnp.sum(received, axis=0)
    entries = 1.0 / (rank * 2 * rank)
    doc_scale = lax.rsqrt(sums[2 * total] * entries + 1e-06)
    query_scale = lax.rsqrt(sums[total : 2 * total] * entries + 1e-06)
    result = sums[:total] * query_scale * (doc_scale / rank)
    return result.reshape(1, 1, total)


def solution(mesh):
    fine = jax.sharding.Mesh(
        mesh.devices.reshape(2, mesh.shape["fsdp"] // 2, mesh.shape["dp"] // 2, 2, 2),
        ("ylo", "z", "x", "core", "yhi"),
    )
    fsdp = ("ylo", "z")
    dp = ("x", "core")
    return jax.shard_map(
        body,
        mesh=fine,
        in_specs=(
            P(fsdp + ("yhi",), None, None),
            P(fsdp + ("yhi",), None, dp),
            P(fsdp + ("yhi",), None, None),
            P(fsdp + ("yhi",), None, dp),
            P(fsdp, dp + ("yhi",)),
            P(fsdp, dp + ("yhi",)),
            P(),
            P(None, dp),
            P(None, dp),
        ),
        out_specs=P(fsdp + ("yhi",), dp, None),
        check_vma=False,
    )
```

```python
import jax
import jax.numpy as jnp
from jax import lax
from jax.sharding import PartitionSpec as P

F32 = jnp.float32
BF16 = jnp.bfloat16

def shift(value, axis, step):
    size = lax.axis_size(axis)
    return lax.ppermute(value, axis, [(i, (i + step) % size) for i in range(size)])


def gathered(weight, piece, cot, early, inner_factor):
    barrier = lax.optimization_barrier
    n_z = lax.axis_size("z")
    z = lax.axis_index("z")
    half = weight.shape[0] // 2
    far_z = (z + n_z // 2) % n_z

    def up(value):
        return shift(value, "z", 1)

    def down(value):
        return shift(value, "z", -1)

    def across(value):
        return shift(value, "ylo", 1)

    def placed(result, by_offset):
        for offset, shard in by_offset:
            result = lax.dynamic_update_slice(result, shard[None], ((z + offset) % n_z, 0, 0))
        return result

    a1, b1, o0, w0, cot, piece, early = barrier(
        (up(weight), down(weight), across(weight), weight, cot, piece, early)
    )
    this_row = placed(
        jnp.zeros((n_z,) + weight.shape, weight.dtype), ((0, w0), (n_z - 1, a1))
    )
    a2, b2, here, o0, cot, own_factor, this_row = barrier(
        (
            up(a1),
            down(b1),
            shift(piece, "yhi", 1),
            o0,
            cot,
            inner_factor(early[0]),
            this_row,
        )
    )
    partner = lax.all_gather(here, ("x", "core"), axis=0, tiled=True)
    a3, b3, oa2, o0, b2 = barrier((up(a2), down(b2), across(a2), o0, b2))
    other_cot = shift(cot, "yhi", 1)
    oa1, ob1, ob2, a4, b4, oa2, other_cot = barrier(
        (up(o0), down(o0), across(b2), up(a3[:half]), down(b3[half:]), oa2, other_cot)
    )
    a4 = jnp.concatenate((a4, b4), axis=0)
    last = (
        (across(a4), far_z),
        (up(oa2), (z + n_z - 3) % n_z),
        (down(ob2), (z + 3) % n_z),
    )
    this_row = placed(
        this_row,
        ((1, b1), (n_z - 2, a2), (2, b2), (n_z - 3, a3), (3, b3), (n_z // 2, a4)),
    )
    other_row = placed(
        jnp.zeros_like(this_row),
        ((0, o0), (n_z - 1, oa1), (1, ob1), (n_z - 2, oa2), (2, ob2)),
    )
    flat = (n_z * weight.shape[0], -1)
    return this_row.reshape(flat), other_row.reshape(flat), last, other_cot, partner, early, own_factor


def projected(pre, cotangent, gate_projection, up_projection):
    cols = pre.shape[1] // 2
    gate = pre[:, :cols]
    up = pre[:, cols:]
    sigma = jax.nn.sigmoid(gate)
    upstream = cotangent.astype(F32)
    gate_grad = (upstream * up * sigma * (1.0 + gate * (1.0 - sigma))).astype(BF16)
    up_grad = (upstream * gate * sigma).astype(BF16)
    dims = (((1,), (1,)), ((), ()))
    return jnp.concatenate(
        (
            lax.dot_general(gate_projection, gate_grad, dims, preferred_element_type=F32),
            lax.dot_general(up_projection, up_grad, dims, preferred_element_type=F32),
        ),
        axis=0,
    )


def body(
    doc_inputs,
    doc_cotangents,
    query_inputs,
    query_cotangents,
    gate_weight,
    up_weight,
    input_projection,
    gate_projection,
    up_projection,
):
    count, length, width = doc_inputs.shape
    half_index = lax.axis_index("yhi")
    row_index = lax.axis_index("ylo")
    dq = ("x", "core", "yhi")
    fsdp = ("ylo", "z")
    n_dq = lax.axis_size(dq)
    n_fsdp = lax.axis_size(fsdp)
    rank = input_projection.shape[0]
    cols = gate_weight.shape[1]

    place = lax.axis_index(("x", "core"))
    piece = jnp.concatenate(
        (
            lax.dynamic_slice_in_dim(doc_inputs, place, 1, 0),
            lax.dynamic_slice_in_dim(query_inputs, place, 1, 0),
        ),
        axis=1,
    )
    own = jnp.concatenate((doc_inputs, query_inputs), axis=1)

    def columns(value, index):
        return lax.dynamic_slice_in_dim(value, index * cols, cols, value.ndim - 1)

    def cotangents(index):
        joined = jnp.concatenate(
            (columns(doc_cotangents, index), columns(query_cotangents, index)), axis=1
        )
        return joined.reshape(-1, cols)

    own_cot = cotangents(half_index)
    weight = jnp.concatenate((gate_weight, up_weight), axis=1)

    def inner_factor(rows):
        return lax.dot_general(
            rows.reshape(-1, width),
            input_projection,
            (((1,), (1,)), ((), ())),
            preferred_element_type=F32,
        )

    this_row, other_row, last, other_cot, other, (own, own_cot), own_factor = gathered(
        weight, piece, cotangents(1 - half_index), (own, own_cot), inner_factor
    )
    gate_proj = columns(gate_projection, half_index)
    up_proj = columns(up_projection, half_index)

    depth = this_row.shape[0]
    shard_depth = weight.shape[0]
    pres = []
    chunks = []
    for rows in (own, other):
        flat = rows.reshape(-1, width)
        this_flat = lax.dynamic_slice_in_dim(flat, row_index * depth, depth, 1)
        other_flat = lax.dynamic_slice_in_dim(flat, (1 - row_index) * depth, depth, 1)
        pre = jnp.dot(this_flat, this_row, preferred_element_type=F32)
        pres.append(pre + jnp.dot(other_flat, other_row, preferred_element_type=F32))
        chunks.append(
            [
                lax.dynamic_slice_in_dim(other_flat, place * shard_depth, shard_depth, 1)
                for _, place in last
            ]
        )
    factors = (own_factor, inner_factor(other))
    shards = [shard for shard, _ in last]
    pres, factors, chunks, shards = lax.optimization_barrier((pres, factors, chunks, shards))
    parts = []
    for pre, pieces, rows_cot in zip(pres, chunks, (own_cot, other_cot)):
        for chunk, shard in zip(pieces, shards):
            pre = pre + jnp.dot(chunk, shard, preferred_element_type=F32)
        parts.append(projected(pre, rows_cot, gate_proj, up_proj))

    first = half_index == 0

    def ordered(pair, axis):
        a = jnp.where(first, pair[0], pair[1])
        b = jnp.where(first, pair[1], pair[0])
        return jnp.concatenate((a, b), axis=axis)

    part = ordered(parts, 1).astype(BF16)
    in_factor = ordered(factors, 0)
    ranks = part.shape[0] // n_dq
    part = part.reshape(n_dq, ranks, -1)
    swapped = lax.all_to_all(part, dq, 0, 0, tiled=True)
    out_sum = jnp.sum(swapped.astype(F32), axis=0)

    pairs = 2 * count
    factor = jnp.einsum(
        "kel,elr->ekr",
        out_sum.reshape(ranks, 2 * pairs, length),
        in_factor.reshape(2 * pairs, length, rank),
        precision=lax.Precision.HIGHEST,
    ).reshape(pairs, 2, ranks * rank)
    docs = factor[:, 0]
    queries = factor[:, 1]
    doc_squares = jnp.sum(docs * docs, axis=1)
    docs = docs.astype(BF16)
    queries = queries.astype(BF16)

    everyone = lax.all_to_all(
        jnp.broadcast_to(queries[None], (n_fsdp,) + queries.shape), fsdp, 0, 0, tiled=True
    ).reshape(n_fsdp * pairs, -1)
    wide = everyone.astype(F32)
    query_squares = jnp.sum(wide * wide, axis=1)
    scores = lax.dot_general(
        docs, everyone, (((1,), (1,)), ((), ())), preferred_element_type=F32
    )
    total = scores.shape[1]

    def to_destinations(x):
        return x.reshape((2, count) + x.shape[1:]).swapaxes(0, 1).reshape(x.shape)

    payload = jnp.concatenate(
        (
            to_destinations(scores),
            jnp.broadcast_to(query_squares[None], (pairs, total)),
            jnp.broadcast_to(to_destinations(doc_squares)[:, None], (pairs, 128)),
        ),
        axis=1,
    )
    received = lax.all_to_all(payload, dq, 0, 0, tiled=True)
    sums = jnp.sum(received, axis=0)
    entries = 1.0 / (rank * 2 * rank)
    doc_scale = lax.rsqrt(sums[2 * total] * entries + 1e-06)
    query_scale = lax.rsqrt(sums[total : 2 * total] * entries + 1e-06)
    result = sums[:total] * query_scale * (doc_scale / rank)
    return result.reshape(1, 1, total)


def solution(mesh):
    fine = jax.sharding.Mesh(
        mesh.devices.reshape(2, mesh.shape["fsdp"] // 2, mesh.shape["dp"] // 2, 2, 2),
        ("ylo", "z", "x", "core", "yhi"),
    )
    fsdp = ("ylo", "z")
    dp = ("x", "core")
    return jax.shard_map(
        body,
        mesh=fine,
        in_specs=(
            P(fsdp + ("yhi",), None, None),
            P(fsdp + ("yhi",), None, dp),
            P(fsdp + ("yhi",), None, None),
            P(fsdp + ("yhi",), None, dp),
            P(fsdp, dp + ("yhi",)),
            P(fsdp, dp + ("yhi",)),
            P(),
            P(None, dp),
            P(None, dp),
        ),
        out_specs=P(fsdp + ("yhi",), dp, None),
        check_vma=False,
    )
```

```python
import jax
import jax.numpy as jnp
from jax import lax
from jax.sharding import PartitionSpec as P

F32 = jnp.float32
BF16 = jnp.bfloat16

def shift(value, axis, step):
    size = lax.axis_size(axis)
    return lax.ppermute(value, axis, [(i, (i + step) % size) for i in range(size)])


def gathered(weight, piece, cot, early, inner_factor, this_product):
    barrier = lax.optimization_barrier
    n_z = lax.axis_size("z")
    z = lax.axis_index("z")
    half = weight.shape[0] // 2
    far_z = (z + n_z // 2) % n_z

    def up(value):
        return shift(value, "z", 1)

    def down(value):
        return shift(value, "z", -1)

    def across(value):
        return shift(value, "ylo", 1)

    def placed(result, by_offset):
        for offset, shard in by_offset:
            result = lax.dynamic_update_slice(result, shard[None], ((z + offset) % n_z, 0, 0))
        return result

    a1, b1, o0, w0, cot, piece, early = barrier(
        (up(weight), down(weight), across(weight), weight, cot, piece, early)
    )
    this_row = placed(
        jnp.zeros((n_z,) + weight.shape, weight.dtype), ((0, w0), (n_z - 1, a1))
    )
    a2, b2, here, o0, cot, own_factor, this_row = barrier(
        (
            up(a1),
            down(b1),
            shift(piece, "yhi", 1),
            o0,
            cot,
            inner_factor(early[0]),
            this_row,
        )
    )
    partner = lax.all_gather(here, ("x", "core"), axis=0, tiled=True)
    a3, b3, oa2, o0, b2 = barrier((up(a2), down(b2), across(a2), o0, b2))
    other_cot = shift(cot, "yhi", 1)
    flat = (n_z * weight.shape[0], -1)
    this_row = placed(this_row, ((1, b1), (n_z - 2, a2), (2, b2), (n_z - 3, a3), (3, b3)))
    this_row = this_row.reshape(flat)
    own_sum = this_product(early[0], this_row)
    oa1, ob1, ob2, a4, b4, oa2, other_cot, own_sum = barrier(
        (
            up(o0),
            down(o0),
            across(b2),
            up(a3[:half]),
            down(b3[half:]),
            oa2,
            other_cot,
            own_sum,
        )
    )
    a4 = jnp.concatenate((a4, b4), axis=0)
    last = (
        (across(a4), far_z),
        (up(oa2), (z + n_z - 3) % n_z),
        (down(ob2), (z + 3) % n_z),
    )
    other_row = placed(
        jnp.zeros((n_z,) + weight.shape, weight.dtype),
        ((0, o0), (n_z - 1, oa1), (1, ob1), (n_z - 2, oa2), (2, ob2)),
    ).reshape(flat)
    own_sum, other_row, partner = barrier((own_sum, other_row, partner))
    this = (this_row, own_sum, (a4, far_z))
    return this, other_row, last, other_cot, partner, early, own_factor


def projected(pre, cotangent, gate_projection, up_projection):
    cols = pre.shape[1] // 2
    gate = pre[:, :cols]
    up = pre[:, cols:]
    sigma = jax.nn.sigmoid(gate)
    upstream = cotangent.astype(F32)
    gate_grad = (upstream * up * sigma * (1.0 + gate * (1.0 - sigma))).astype(BF16)
    up_grad = (upstream * gate * sigma).astype(BF16)
    dims = (((1,), (1,)), ((), ()))
    return jnp.concatenate(
        (
            lax.dot_general(gate_projection, gate_grad, dims, preferred_element_type=F32),
            lax.dot_general(up_projection, up_grad, dims, preferred_element_type=F32),
        ),
        axis=0,
    )


def body(
    doc_inputs,
    doc_cotangents,
    query_inputs,
    query_cotangents,
    gate_weight,
    up_weight,
    input_projection,
    gate_projection,
    up_projection,
):
    count, length, width = doc_inputs.shape
    half_index = lax.axis_index("yhi")
    row_index = lax.axis_index("ylo")
    dq = ("x", "core", "yhi")
    fsdp = ("ylo", "z")
    n_dq = lax.axis_size(dq)
    n_fsdp = lax.axis_size(fsdp)
    rank = input_projection.shape[0]
    cols = gate_weight.shape[1]

    place = lax.axis_index(("x", "core"))
    piece = jnp.concatenate(
        (
            lax.dynamic_slice_in_dim(doc_inputs, place, 1, 0),
            lax.dynamic_slice_in_dim(query_inputs, place, 1, 0),
        ),
        axis=1,
    )
    own = jnp.concatenate((doc_inputs, query_inputs), axis=1)

    def columns(value, index):
        return lax.dynamic_slice_in_dim(value, index * cols, cols, value.ndim - 1)

    def cotangents(index):
        joined = jnp.concatenate(
            (columns(doc_cotangents, index), columns(query_cotangents, index)), axis=1
        )
        return joined.reshape(-1, cols)

    own_cot = cotangents(half_index)
    weight = jnp.concatenate((gate_weight, up_weight), axis=1)

    def inner_factor(rows):
        return lax.dot_general(
            rows.reshape(-1, width),
            input_projection,
            (((1,), (1,)), ((), ())),
            preferred_element_type=F32,
        )

    def half_of(rows, side, depth):
        return lax.dynamic_slice_in_dim(rows.reshape(-1, width), side * depth, depth, 1)

    def this_product(rows, this_row):
        flat = half_of(rows, row_index, this_row.shape[0])
        return jnp.dot(flat, this_row, preferred_element_type=F32)

    this, other_row, last, other_cot, other, (own, own_cot), own_factor = gathered(
        weight, piece, cotangents(1 - half_index), (own, own_cot), inner_factor, this_product
    )
    this_row, own_sum, far = this
    gate_proj = columns(gate_projection, half_index)
    up_proj = columns(up_projection, half_index)

    depth = this_row.shape[0]
    shard_depth = weight.shape[0]

    def chunk(rows, side, place):
        return lax.dynamic_slice_in_dim(
            rows.reshape(-1, width), side * depth + place * shard_depth, shard_depth, 1
        )

    def rest(rows, pre):
        pre = pre + jnp.dot(
            half_of(rows, 1 - row_index, depth), other_row, preferred_element_type=F32
        )
        return pre + jnp.dot(
            chunk(rows, row_index, far[1]), far[0], preferred_element_type=F32
        )

    own_pre = rest(own, own_sum)
    own_pre, other = lax.optimization_barrier((own_pre, other))
    pres = (own_pre, rest(other, this_product(other, this_row)))
    chunks = [[chunk(rows, 1 - row_index, at) for _, at in last] for rows in (own, other)]
    factors = (own_factor, inner_factor(other))
    shards = [shard for shard, _ in last]
    factors = (own_factor, inner_factor(other))
    shards = [shard for shard, _ in last]
    pres, factors, chunks, shards = lax.optimization_barrier((pres, factors, chunks, shards))
    parts = []
    for pre, pieces, rows_cot in zip(pres, chunks, (own_cot, other_cot)):
        for chunk, shard in zip(pieces, shards):
            pre = pre + jnp.dot(chunk, shard, preferred_element_type=F32)
        parts.append(projected(pre, rows_cot, gate_proj, up_proj))

    first = half_index == 0

    def ordered(pair, axis):
        a = jnp.where(first, pair[0], pair[1])
        b = jnp.where(first, pair[1], pair[0])
        return jnp.concatenate((a, b), axis=axis)

    part = ordered(parts, 1).astype(BF16)
    in_factor = ordered(factors, 0)
    ranks = part.shape[0] // n_dq
    part = part.reshape(n_dq, ranks, -1)
    swapped = lax.all_to_all(part, dq, 0, 0, tiled=True)
    out_sum = jnp.sum(swapped.astype(F32), axis=0)

    pairs = 2 * count
    factor = jnp.einsum(
        "kel,elr->ekr",
        out_sum.reshape(ranks, 2 * pairs, length),
        in_factor.reshape(2 * pairs, length, rank),
        precision=lax.Precision.HIGHEST,
    ).reshape(pairs, 2, ranks * rank)
    docs = factor[:, 0]
    queries = factor[:, 1]
    doc_squares = jnp.sum(docs * docs, axis=1)
    docs = docs.astype(BF16)
    queries = queries.astype(BF16)

    everyone = lax.all_to_all(
        jnp.broadcast_to(queries[None], (n_fsdp,) + queries.shape), fsdp, 0, 0, tiled=True
    ).reshape(n_fsdp * pairs, -1)
    wide = everyone.astype(F32)
    query_squares = jnp.sum(wide * wide, axis=1)
    scores = lax.dot_general(
        docs, everyone, (((1,), (1,)), ((), ())), preferred_element_type=F32
    )
    total = scores.shape[1]

    def to_destinations(x):
        return x.reshape((2, count) + x.shape[1:]).swapaxes(0, 1).reshape(x.shape)

    payload = jnp.concatenate(
        (
            to_destinations(scores),
            jnp.broadcast_to(query_squares[None], (pairs, total)),
            jnp.broadcast_to(to_destinations(doc_squares)[:, None], (pairs, 128)),
        ),
        axis=1,
    )
    received = lax.all_to_all(payload, dq, 0, 0, tiled=True)
    sums = jnp.sum(received, axis=0)
    entries = 1.0 / (rank * 2 * rank)
    doc_scale = lax.rsqrt(sums[2 * total] * entries + 1e-06)
    query_scale = lax.rsqrt(sums[total : 2 * total] * entries + 1e-06)
    result = sums[:total] * query_scale * (doc_scale / rank)
    return result.reshape(1, 1, total)


def solution(mesh):
    fine = jax.sharding.Mesh(
        mesh.devices.reshape(2, mesh.shape["fsdp"] // 2, mesh.shape["dp"] // 2, 2, 2),
        ("ylo", "z", "x", "core", "yhi"),
    )
    fsdp = ("ylo", "z")
    dp = ("x", "core")
    return jax.shard_map(
        body,
        mesh=fine,
        in_specs=(
            P(fsdp + ("yhi",), None, None),
            P(fsdp + ("yhi",), None, dp),
            P(fsdp + ("yhi",), None, None),
            P(fsdp + ("yhi",), None, dp),
            P(fsdp, dp + ("yhi",)),
            P(fsdp, dp + ("yhi",)),
            P(),
            P(None, dp),
            P(None, dp),
        ),
        out_specs=P(fsdp + ("yhi",), dp, None),
        check_vma=False,
    )
```

```python
import jax
import jax.numpy as jnp
from jax import lax
from jax.sharding import PartitionSpec as P

F32 = jnp.float32
BF16 = jnp.bfloat16

def shift(value, axis, step):
    size = lax.axis_size(axis)
    return lax.ppermute(value, axis, [(i, (i + step) % size) for i in range(size)])


def gathered(weight, piece, cot, early, inner_factor, this_product):
    barrier = lax.optimization_barrier
    n_z = lax.axis_size("z")
    z = lax.axis_index("z")
    half = weight.shape[0] // 2
    far_z = (z + n_z // 2) % n_z

    def up(value):
        return shift(value, "z", 1)

    def down(value):
        return shift(value, "z", -1)

    def across(value):
        return shift(value, "ylo", 1)

    def placed(result, by_offset):
        for offset, shard in by_offset:
            result = lax.dynamic_update_slice(result, shard[None], ((z + offset) % n_z, 0, 0))
        return result

    a1, b1, o0, w0, cot, piece, early = barrier(
        (up(weight), down(weight), across(weight), weight, cot, piece, early)
    )
    this_row = placed(
        jnp.zeros((n_z,) + weight.shape, weight.dtype), ((0, w0), (n_z - 1, a1))
    )
    a2, b2, here, o0, cot, own_factor, this_row = barrier(
        (
            up(a1),
            down(b1),
            shift(piece, "yhi", 1),
            o0,
            cot,
            inner_factor(early[0]),
            this_row,
        )
    )
    partner = lax.all_gather(here, ("x", "core"), axis=0, tiled=True)
    a3, b3, oa2, o0, b2 = barrier((up(a2), down(b2), across(a2), o0, b2))
    other_cot = shift(cot, "yhi", 1)
    flat = (n_z * weight.shape[0], -1)
    this_row = placed(this_row, ((1, b1), (n_z - 2, a2), (2, b2), (n_z - 3, a3), (3, b3)))
    this_row = this_row.reshape(flat)
    own_sum = this_product(early[0], this_row)
    oa1, ob1, ob2, a4, b4, oa2, other_cot, own_sum = barrier(
        (
            up(o0),
            down(o0),
            across(b2),
            up(a3[:half]),
            down(b3[half:]),
            oa2,
            other_cot,
            own_sum,
        )
    )
    a4 = jnp.concatenate((a4, b4), axis=0)
    last = (
        (across(a4), far_z),
        (up(oa2), (z + n_z - 3) % n_z),
        (down(ob2), (z + 3) % n_z),
    )
    other_row = placed(
        jnp.zeros((n_z,) + weight.shape, weight.dtype),
        ((0, o0), (n_z - 1, oa1), (1, ob1), (n_z - 2, oa2), (2, ob2)),
    ).reshape(flat)
    this = (this_row, own_sum, (a4, far_z))
    return this, other_row, last, other_cot, partner, early, own_factor


def projected(pre, cotangent, gate_projection, up_projection):
    cols = pre.shape[1] // 2
    gate = pre[:, :cols]
    up = pre[:, cols:]
    sigma = jax.nn.sigmoid(gate)
    upstream = cotangent.astype(F32)
    gate_grad = (upstream * up * sigma * (1.0 + gate * (1.0 - sigma))).astype(BF16)
    up_grad = (upstream * gate * sigma).astype(BF16)
    dims = (((1,), (1,)), ((), ()))
    return jnp.concatenate(
        (
            lax.dot_general(gate_projection, gate_grad, dims, preferred_element_type=F32),
            lax.dot_general(up_projection, up_grad, dims, preferred_element_type=F32),
        ),
        axis=0,
    )


def body(
    doc_inputs,
    doc_cotangents,
    query_inputs,
    query_cotangents,
    gate_weight,
    up_weight,
    input_projection,
    gate_projection,
    up_projection,
):
    count, length, width = doc_inputs.shape
    half_index = lax.axis_index("yhi")
    row_index = lax.axis_index("ylo")
    dq = ("x", "core", "yhi")
    fsdp = ("ylo", "z")
    n_dq = lax.axis_size(dq)
    n_fsdp = lax.axis_size(fsdp)
    rank = input_projection.shape[0]
    cols = gate_weight.shape[1]

    place = lax.axis_index(("x", "core"))
    piece = jnp.concatenate(
        (
            lax.dynamic_slice_in_dim(doc_inputs, place, 1, 0),
            lax.dynamic_slice_in_dim(query_inputs, place, 1, 0),
        ),
        axis=1,
    )
    own = jnp.concatenate((doc_inputs, query_inputs), axis=1)

    def columns(value, index):
        return lax.dynamic_slice_in_dim(value, index * cols, cols, value.ndim - 1)

    def cotangents(index):
        joined = jnp.concatenate(
            (columns(doc_cotangents, index), columns(query_cotangents, index)), axis=1
        )
        return joined.reshape(-1, cols)

    own_cot = cotangents(half_index)
    weight = jnp.concatenate((gate_weight, up_weight), axis=1)

    def inner_factor(rows):
        return lax.dot_general(
            rows.reshape(-1, width),
            input_projection,
            (((1,), (1,)), ((), ())),
            preferred_element_type=F32,
        )

    def half_of(rows, side, depth):
        return lax.dynamic_slice_in_dim(rows.reshape(-1, width), side * depth, depth, 1)

    def this_product(rows, this_row):
        flat = half_of(rows, row_index, this_row.shape[0])
        return jnp.dot(flat, this_row, preferred_element_type=F32)

    this, other_row, last, other_cot, other, (own, own_cot), own_factor = gathered(
        weight, piece, cotangents(1 - half_index), (own, own_cot), inner_factor, this_product
    )
    this_row, own_sum, far = this
    gate_proj = columns(gate_projection, half_index)
    up_proj = columns(up_projection, half_index)

    depth = this_row.shape[0]
    shard_depth = weight.shape[0]

    def chunk(rows, side, place):
        return lax.dynamic_slice_in_dim(
            rows.reshape(-1, width), side * depth + place * shard_depth, shard_depth, 1
        )

    def rest(rows, pre):
        pre = pre + jnp.dot(
            half_of(rows, 1 - row_index, depth), other_row, preferred_element_type=F32
        )
        return pre + jnp.dot(
            chunk(rows, row_index, far[1]), far[0], preferred_element_type=F32
        )

    pres = (rest(own, own_sum), rest(other, this_product(other, this_row)))
    chunks = [[chunk(rows, 1 - row_index, at) for _, at in last] for rows in (own, other)]
    factors = (own_factor, inner_factor(other))
    shards = [shard for shard, _ in last]
    factors = (own_factor, inner_factor(other))
    shards = [shard for shard, _ in last]
    pres, factors, chunks, shards = lax.optimization_barrier((pres, factors, chunks, shards))
    parts = []
    for pre, pieces, rows_cot in zip(pres, chunks, (own_cot, other_cot)):
        for chunk, shard in zip(pieces, shards):
            pre = pre + jnp.dot(chunk, shard, preferred_element_type=F32)
        parts.append(projected(pre, rows_cot, gate_proj, up_proj))

    first = half_index == 0

    def ordered(pair, axis):
        a = jnp.where(first, pair[0], pair[1])
        b = jnp.where(first, pair[1], pair[0])
        return jnp.concatenate((a, b), axis=axis)

    part = ordered(parts, 1).astype(BF16)
    in_factor = ordered(factors, 0)
    ranks = part.shape[0] // n_dq
    part = part.reshape(n_dq, ranks, -1)
    swapped = lax.all_to_all(part, dq, 0, 0, tiled=True)
    out_sum = jnp.sum(swapped.astype(F32), axis=0)

    pairs = 2 * count
    factor = jnp.einsum(
        "kel,elr->ekr",
        out_sum.reshape(ranks, 2 * pairs, length),
        in_factor.reshape(2 * pairs, length, rank),
        precision=lax.Precision.HIGHEST,
    ).reshape(pairs, 2, ranks * rank)
    docs = factor[:, 0]
    queries = factor[:, 1]
    doc_squares = jnp.sum(docs * docs, axis=1)
    docs = docs.astype(BF16)
    queries = queries.astype(BF16)

    everyone = lax.all_to_all(
        jnp.broadcast_to(queries[None], (n_fsdp,) + queries.shape), fsdp, 0, 0, tiled=True
    ).reshape(n_fsdp * pairs, -1)
    wide = everyone.astype(F32)
    query_squares = jnp.sum(wide * wide, axis=1)
    scores = lax.dot_general(
        docs, everyone, (((1,), (1,)), ((), ())), preferred_element_type=F32
    )
    total = scores.shape[1]

    def to_destinations(x):
        return x.reshape((2, count) + x.shape[1:]).swapaxes(0, 1).reshape(x.shape)

    payload = jnp.concatenate(
        (
            to_destinations(scores),
            jnp.broadcast_to(query_squares[None], (pairs, total)),
            jnp.broadcast_to(to_destinations(doc_squares)[:, None], (pairs, 128)),
        ),
        axis=1,
    )
    received = lax.all_to_all(payload, dq, 0, 0, tiled=True)
    sums = jnp.sum(received, axis=0)
    entries = 1.0 / (rank * 2 * rank)
    doc_scale = lax.rsqrt(sums[2 * total] * entries + 1e-06)
    query_scale = lax.rsqrt(sums[total : 2 * total] * entries + 1e-06)
    result = sums[:total] * query_scale * (doc_scale / rank)
    return result.reshape(1, 1, total)


def solution(mesh):
    fine = jax.sharding.Mesh(
        mesh.devices.reshape(2, mesh.shape["fsdp"] // 2, mesh.shape["dp"] // 2, 2, 2),
        ("ylo", "z", "x", "core", "yhi"),
    )
    fsdp = ("ylo", "z")
    dp = ("x", "core")
    return jax.shard_map(
        body,
        mesh=fine,
        in_specs=(
            P(fsdp + ("yhi",), None, None),
            P(fsdp + ("yhi",), None, dp),
            P(fsdp + ("yhi",), None, None),
            P(fsdp + ("yhi",), None, dp),
            P(fsdp, dp + ("yhi",)),
            P(fsdp, dp + ("yhi",)),
            P(),
            P(None, dp),
            P(None, dp),
        ),
        out_specs=P(fsdp + ("yhi",), dp, None),
        check_vma=False,
    )
```

```python
import jax
import jax.numpy as jnp
from jax import lax
from jax.experimental import pallas as pl
from jax.experimental.pallas import tpu as pltpu
from jax.sharding import PartitionSpec as P

F32 = jnp.float32
BF16 = jnp.bfloat16

def shift(value, axis, step):
    size = lax.axis_size(axis)
    return lax.ppermute(value, axis, [(i, (i + step) % size) for i in range(size)])


def gathered(weight, piece, cot, early, inner_factor):
    barrier = lax.optimization_barrier
    n_z = lax.axis_size("z")
    z = lax.axis_index("z")
    half = weight.shape[0] // 2
    far_z = (z + n_z // 2) % n_z

    def up(value):
        return shift(value, "z", 1)

    def down(value):
        return shift(value, "z", -1)

    def across(value):
        return shift(value, "ylo", 1)

    def placed(result, by_offset):
        for offset, shard in by_offset:
            result = lax.dynamic_update_slice(result, shard[None], ((z + offset) % n_z, 0, 0))
        return result

    a1, b1, o0, w0, cot, piece, early = barrier(
        (up(weight), down(weight), across(weight), weight, cot, piece, early)
    )
    this_row = placed(
        jnp.zeros((n_z,) + weight.shape, weight.dtype), ((0, w0), (n_z - 1, a1))
    )
    a2, b2, here, o0, cot, own_factor, this_row = barrier(
        (
            up(a1),
            down(b1),
            shift(piece, "yhi", 1),
            o0,
            cot,
            inner_factor(early[0]),
            this_row,
        )
    )
    partner = lax.all_gather(here, ("x", "core"), axis=0, tiled=True)
    a3, b3, oa2, o0, b2 = barrier((up(a2), down(b2), across(a2), o0, b2))
    other_cot = shift(cot, "yhi", 1)
    oa1, ob1, ob2, a4, b4, oa2, other_cot = barrier(
        (up(o0), down(o0), across(b2), up(a3[:half]), down(b3[half:]), oa2, other_cot)
    )
    a4 = jnp.concatenate((a4, b4), axis=0)
    last = (
        (across(a4), far_z),
        (up(oa2), (z + n_z - 3) % n_z),
        (down(ob2), (z + 3) % n_z),
    )
    this_row = placed(
        this_row,
        ((1, b1), (n_z - 2, a2), (2, b2), (n_z - 3, a3), (3, b3), (n_z // 2, a4)),
    )
    other_row = placed(
        jnp.zeros_like(this_row),
        ((0, o0), (n_z - 1, oa1), (1, ob1), (n_z - 2, oa2), (2, ob2)),
    )
    flat = (n_z * weight.shape[0], -1)
    return this_row.reshape(flat), other_row.reshape(flat), last, other_cot, partner, early, own_factor


VMEM_LIMIT = 14 * 2**20
ROWS = 256
WHOLE = pl.BlockSpec(memory_space=pltpu.VMEM)


def halves_kernel(side_ref, this_x, other_x, this_row, other_row, out):
    del side_ref
    out[...] = jnp.dot(
        this_x[...], this_row[...], preferred_element_type=F32
    ) + jnp.dot(other_x[...], other_row[...], preferred_element_type=F32)


def halves_product(rows, this_row, other_row, row_index):
    count, width = rows.shape
    depth, cols = this_row.shape
    return pl.pallas_call(
        halves_kernel,
        out_shape=jax.ShapeDtypeStruct((count, cols), F32),
        grid_spec=pltpu.PrefetchScalarGridSpec(
            num_scalar_prefetch=1,
            grid=(count // ROWS,),
            in_specs=[
                pl.BlockSpec((ROWS, depth), lambda i, side: (i, side[0])),
                pl.BlockSpec((ROWS, depth), lambda i, side: (i, 1 - side[0])),
                WHOLE,
                WHOLE,
            ],
            out_specs=pl.BlockSpec((ROWS, cols), lambda i, side: (i, 0)),
        ),
        compiler_params=pltpu.CompilerParams(vmem_limit_bytes=VMEM_LIMIT),
        cost_estimate=pl.CostEstimate(
            flops=2 * count * width * cols,
            bytes_accessed=2 * count * width + 4 * count * cols,
            transcendentals=0,
        ),
        name="halves_product",
    )(row_index.astype(jnp.int32).reshape(1), rows, rows, this_row, other_row)


def projected(pre, cotangent, gate_projection, up_projection):
    cols = pre.shape[1] // 2
    gate = pre[:, :cols]
    up = pre[:, cols:]
    sigma = jax.nn.sigmoid(gate)
    upstream = cotangent.astype(F32)
    gate_grad = (upstream * up * sigma * (1.0 + gate * (1.0 - sigma))).astype(BF16)
    up_grad = (upstream * gate * sigma).astype(BF16)
    dims = (((1,), (1,)), ((), ()))
    return jnp.concatenate(
        (
            lax.dot_general(gate_projection, gate_grad, dims, preferred_element_type=F32),
            lax.dot_general(up_projection, up_grad, dims, preferred_element_type=F32),
        ),
        axis=0,
    )


def body(
    doc_inputs,
    doc_cotangents,
    query_inputs,
    query_cotangents,
    gate_weight,
    up_weight,
    input_projection,
    gate_projection,
    up_projection,
):
    count, length, width = doc_inputs.shape
    half_index = lax.axis_index("yhi")
    row_index = lax.axis_index("ylo")
    dq = ("x", "core", "yhi")
    fsdp = ("ylo", "z")
    n_dq = lax.axis_size(dq)
    n_fsdp = lax.axis_size(fsdp)
    rank = input_projection.shape[0]
    cols = gate_weight.shape[1]

    place = lax.axis_index(("x", "core"))
    piece = jnp.concatenate(
        (
            lax.dynamic_slice_in_dim(doc_inputs, place, 1, 0),
            lax.dynamic_slice_in_dim(query_inputs, place, 1, 0),
        ),
        axis=1,
    )
    own = jnp.concatenate((doc_inputs, query_inputs), axis=1)

    def columns(value, index):
        return lax.dynamic_slice_in_dim(value, index * cols, cols, value.ndim - 1)

    def cotangents(index):
        joined = jnp.concatenate(
            (columns(doc_cotangents, index), columns(query_cotangents, index)), axis=1
        )
        return joined.reshape(-1, cols)

    own_cot = cotangents(half_index)
    weight = jnp.concatenate((gate_weight, up_weight), axis=1)

    def inner_factor(rows):
        return lax.dot_general(
            rows.reshape(-1, width),
            input_projection,
            (((1,), (1,)), ((), ())),
            preferred_element_type=F32,
        )

    this_row, other_row, last, other_cot, other, (own, own_cot), own_factor = gathered(
        weight, piece, cotangents(1 - half_index), (own, own_cot), inner_factor
    )
    gate_proj = columns(gate_projection, half_index)
    up_proj = columns(up_projection, half_index)

    depth = this_row.shape[0]
    shard_depth = weight.shape[0]
    pres = []
    chunks = []
    for rows in (own, other):
        flat = rows.reshape(-1, width)
        other_flat = lax.dynamic_slice_in_dim(flat, (1 - row_index) * depth, depth, 1)
        if rows is own:
            this_flat = lax.dynamic_slice_in_dim(flat, row_index * depth, depth, 1)
            pre = jnp.dot(this_flat, this_row, preferred_element_type=F32)
            pre = pre + jnp.dot(other_flat, other_row, preferred_element_type=F32)
        else:
            pre = halves_product(flat, this_row, other_row, row_index)
        pres.append(pre)
        chunks.append(
            [
                lax.dynamic_slice_in_dim(other_flat, place * shard_depth, shard_depth, 1)
                for _, place in last
            ]
        )
    factors = (own_factor, inner_factor(other))
    shards = [shard for shard, _ in last]
    pres, factors, chunks, shards = lax.optimization_barrier((pres, factors, chunks, shards))
    parts = []
    for pre, pieces, rows_cot in zip(pres, chunks, (own_cot, other_cot)):
        for chunk, shard in zip(pieces, shards):
            pre = pre + jnp.dot(chunk, shard, preferred_element_type=F32)
        parts.append(projected(pre, rows_cot, gate_proj, up_proj))

    first = half_index == 0

    def ordered(pair, axis):
        a = jnp.where(first, pair[0], pair[1])
        b = jnp.where(first, pair[1], pair[0])
        return jnp.concatenate((a, b), axis=axis)

    part = ordered(parts, 1)
    in_factor = ordered(factors, 0)
    ranks = part.shape[0] // n_dq
    core = lax.axis_index("core")
    part = part.reshape(2, n_dq // 2, ranks, -1)
    mine = lax.dynamic_index_in_dim(part, core, 0, keepdims=False)
    theirs = lax.dynamic_index_in_dim(part, 1 - core, 0, keepdims=False)
    part = (mine + shift(theirs, "core", 1)).astype(BF16)
    swapped = lax.all_to_all(part, ("x", "yhi"), 0, 0, tiled=True)
    out_sum = jnp.sum(swapped.astype(F32), axis=0)

    pairs = 2 * count
    factor = jnp.einsum(
        "kel,elr->ekr",
        out_sum.reshape(ranks, 2 * pairs, length),
        in_factor.reshape(2 * pairs, length, rank),
        precision=lax.Precision.HIGHEST,
    ).reshape(pairs, 2, ranks * rank)
    docs = factor[:, 0]
    queries = factor[:, 1]
    doc_squares = jnp.sum(docs * docs, axis=1)
    docs = docs.astype(BF16)
    queries = queries.astype(BF16)

    everyone = lax.all_to_all(
        jnp.broadcast_to(queries[None], (n_fsdp,) + queries.shape), fsdp, 0, 0, tiled=True
    ).reshape(n_fsdp * pairs, -1)
    wide = everyone.astype(F32)
    query_squares = jnp.sum(wide * wide, axis=1)
    scores = lax.dot_general(
        docs, everyone, (((1,), (1,)), ((), ())), preferred_element_type=F32
    )
    total = scores.shape[1]

    def to_destinations(x):
        return x.reshape((2, count) + x.shape[1:]).swapaxes(0, 1).reshape(x.shape)

    payload = jnp.concatenate(
        (
            to_destinations(scores),
            jnp.broadcast_to(query_squares[None], (pairs, total)),
            jnp.broadcast_to(to_destinations(doc_squares)[:, None], (pairs, 128)),
        ),
        axis=1,
    )
    received = lax.all_to_all(payload, dq, 0, 0, tiled=True)
    sums = jnp.sum(received, axis=0)
    entries = 1.0 / (rank * 2 * rank)
    doc_scale = lax.rsqrt(sums[2 * total] * entries + 1e-06)
    query_scale = lax.rsqrt(sums[total : 2 * total] * entries + 1e-06)
    result = sums[:total] * query_scale * (doc_scale / rank)
    return result.reshape(1, 1, total)


def solution(mesh):
    fine = jax.sharding.Mesh(
        mesh.devices.reshape(2, mesh.shape["fsdp"] // 2, mesh.shape["dp"] // 2, 2, 2),
        ("ylo", "z", "x", "core", "yhi"),
    )
    fsdp = ("ylo", "z")
    dp = ("x", "core")
    return jax.shard_map(
        body,
        mesh=fine,
        in_specs=(
            P(fsdp + ("yhi",), None, None),
            P(fsdp + ("yhi",), None, dp),
            P(fsdp + ("yhi",), None, None),
            P(fsdp + ("yhi",), None, dp),
            P(fsdp, dp + ("yhi",)),
            P(fsdp, dp + ("yhi",)),
            P(),
            P(None, dp),
            P(None, dp),
        ),
        out_specs=P(fsdp + ("yhi",), dp, None),
        check_vma=False,
    )
```

```python
import jax
import jax.numpy as jnp
from jax import lax
from jax.sharding import PartitionSpec as P

F32 = jnp.float32
BF16 = jnp.bfloat16

def shift(value, axis, step):
    size = lax.axis_size(axis)
    return lax.ppermute(value, axis, [(i, (i + step) % size) for i in range(size)])


def gathered(weight, piece, cot, early, inner_factor):
    barrier = lax.optimization_barrier
    n_z = lax.axis_size("z")
    z = lax.axis_index("z")
    half = weight.shape[0] // 2

    def up(value):
        return shift(value, "z", 1)

    def down(value):
        return shift(value, "z", -1)

    def across(value):
        return shift(value, "ylo", 1)

    this = lax.axis_index("ylo") * n_z
    other = n_z - this

    def placed(result, by_offset):
        for side, offset, shard in by_offset:
            at = side + (z + offset) % n_z
            result = lax.dynamic_update_slice(result, shard[None], (at, 0, 0))
        return result

    a1, b1, o0, w0, cot, piece, early = barrier(
        (up(weight), down(weight), across(weight), weight, cot, piece, early)
    )
    joined = placed(
        jnp.zeros((2 * n_z,) + weight.shape, weight.dtype), ((this, 0, w0), (this, n_z - 1, a1))
    )
    a2, b2, here, o0, cot, own_factor, joined = barrier(
        (
            up(a1),
            down(b1),
            shift(piece, "yhi", 1),
            o0,
            cot,
            inner_factor(early[0]),
            joined,
        )
    )
    partner = lax.all_gather(here, ("x", "core"), axis=0, tiled=True)
    a3, b3, oa2, o0, b2 = barrier((up(a2), down(b2), across(a2), o0, b2))
    other_cot = shift(cot, "yhi", 1)
    oa1, ob1, ob2, a4, b4, oa2, other_cot = barrier(
        (up(o0), down(o0), across(b2), up(a3[:half]), down(b3[half:]), oa2, other_cot)
    )
    a4 = jnp.concatenate((a4, b4), axis=0)
    last = (
        (across(a4), other + (z + n_z // 2) % n_z),
        (up(oa2), other + (z + n_z - 3) % n_z),
        (down(ob2), other + (z + 3) % n_z),
    )
    joined = placed(
        joined,
        (
            (this, 1, b1),
            (other, 0, o0),
            (this, n_z - 2, a2),
            (this, 2, b2),
            (this, n_z - 3, a3),
            (this, 3, b3),
            (other, n_z - 2, oa2),
            (this, n_z // 2, a4),
            (other, n_z - 1, oa1),
            (other, 1, ob1),
            (other, 2, ob2),
        ),
    )
    joined = joined.reshape(2 * n_z * weight.shape[0], -1)
    return joined, last, other_cot, partner, early, own_factor


def projected(pre, cotangent, gate_projection, up_projection):
    cols = pre.shape[1] // 2
    gate = pre[:, :cols]
    up = pre[:, cols:]
    sigma = jax.nn.sigmoid(gate)
    upstream = cotangent.astype(F32)
    gate_grad = (upstream * up * sigma * (1.0 + gate * (1.0 - sigma))).astype(BF16)
    up_grad = (upstream * gate * sigma).astype(BF16)
    dims = (((1,), (1,)), ((), ()))
    return jnp.concatenate(
        (
            lax.dot_general(gate_projection, gate_grad, dims, preferred_element_type=F32),
            lax.dot_general(up_projection, up_grad, dims, preferred_element_type=F32),
        ),
        axis=0,
    )


def body(
    doc_inputs,
    doc_cotangents,
    query_inputs,
    query_cotangents,
    gate_weight,
    up_weight,
    input_projection,
    gate_projection,
    up_projection,
):
    count, length, width = doc_inputs.shape
    half_index = lax.axis_index("yhi")
    dq = ("x", "core", "yhi")
    fsdp = ("ylo", "z")
    n_dq = lax.axis_size(dq)
    n_fsdp = lax.axis_size(fsdp)
    rank = input_projection.shape[0]
    cols = gate_weight.shape[1]

    place = lax.axis_index(("x", "core"))
    piece = jnp.concatenate(
        (
            lax.dynamic_slice_in_dim(doc_inputs, place, 1, 0),
            lax.dynamic_slice_in_dim(query_inputs, place, 1, 0),
        ),
        axis=1,
    )
    own = jnp.concatenate((doc_inputs, query_inputs), axis=1)

    def columns(value, index):
        return lax.dynamic_slice_in_dim(value, index * cols, cols, value.ndim - 1)

    def cotangents(index):
        joined = jnp.concatenate(
            (columns(doc_cotangents, index), columns(query_cotangents, index)), axis=1
        )
        return joined.reshape(-1, cols)

    own_cot = cotangents(half_index)
    weight = jnp.concatenate((gate_weight, up_weight), axis=1)

    def inner_factor(rows):
        return lax.dot_general(
            rows.reshape(-1, width),
            input_projection,
            (((1,), (1,)), ((), ())),
            preferred_element_type=F32,
        )

    joined, last, other_cot, other, (own, own_cot), own_factor = gathered(
        weight, piece, cotangents(1 - half_index), (own, own_cot), inner_factor
    )
    gate_proj = columns(gate_projection, half_index)
    up_proj = columns(up_projection, half_index)

    depth = weight.shape[0]
    pres = []
    chunks = []
    for rows in (own, other):
        flat = rows.reshape(-1, width)
        pres.append(jnp.dot(flat, joined, preferred_element_type=F32))
        chunks.append([lax.dynamic_slice_in_dim(flat, at * depth, depth, 1) for _, at in last])
    factors = (own_factor, inner_factor(other))
    shards = [shard for shard, _ in last]
    pres, factors, chunks, shards = lax.optimization_barrier((pres, factors, chunks, shards))
    parts = []
    for pre, pieces, rows_cot in zip(pres, chunks, (own_cot, other_cot)):
        for chunk, shard in zip(pieces, shards):
            pre = pre + jnp.dot(chunk, shard, preferred_element_type=F32)
        parts.append(projected(pre, rows_cot, gate_proj, up_proj))

    first = half_index == 0

    def ordered(pair, axis):
        a = jnp.where(first, pair[0], pair[1])
        b = jnp.where(first, pair[1], pair[0])
        return jnp.concatenate((a, b), axis=axis)

    part = ordered(parts, 1).astype(BF16)
    in_factor = ordered(factors, 0)
    ranks = part.shape[0] // n_dq
    part = part.reshape(n_dq, ranks, -1)
    swapped = lax.all_to_all(part, dq, 0, 0, tiled=True)
    out_sum = jnp.sum(swapped.astype(F32), axis=0)

    pairs = 2 * count
    factor = jnp.einsum(
        "kel,elr->ekr",
        out_sum.reshape(ranks, 2 * pairs, length),
        in_factor.reshape(2 * pairs, length, rank),
        precision=lax.Precision.HIGHEST,
    ).reshape(pairs, 2, ranks * rank)
    docs = factor[:, 0]
    queries = factor[:, 1]
    doc_squares = jnp.sum(docs * docs, axis=1)
    docs = docs.astype(BF16)
    queries = queries.astype(BF16)

    everyone = lax.all_to_all(
        jnp.broadcast_to(queries[None], (n_fsdp,) + queries.shape), fsdp, 0, 0, tiled=True
    ).reshape(n_fsdp * pairs, -1)
    wide = everyone.astype(F32)
    query_squares = jnp.sum(wide * wide, axis=1)
    scores = lax.dot_general(
        docs, everyone, (((1,), (1,)), ((), ())), preferred_element_type=F32
    )
    total = scores.shape[1]

    def to_destinations(x):
        return x.reshape((2, count) + x.shape[1:]).swapaxes(0, 1).reshape(x.shape)

    payload = jnp.concatenate(
        (
            to_destinations(scores),
            jnp.broadcast_to(query_squares[None], (pairs, total)),
            jnp.broadcast_to(to_destinations(doc_squares)[:, None], (pairs, 128)),
        ),
        axis=1,
    )
    received = lax.all_to_all(payload, dq, 0, 0, tiled=True)
    sums = jnp.sum(received, axis=0)
    entries = 1.0 / (rank * 2 * rank)
    doc_scale = lax.rsqrt(sums[2 * total] * entries + 1e-06)
    query_scale = lax.rsqrt(sums[total : 2 * total] * entries + 1e-06)
    result = sums[:total] * query_scale * (doc_scale / rank)
    return result.reshape(1, 1, total)


def solution(mesh):
    fine = jax.sharding.Mesh(
        mesh.devices.reshape(2, mesh.shape["fsdp"] // 2, mesh.shape["dp"] // 2, 2, 2),
        ("ylo", "z", "x", "core", "yhi"),
    )
    fsdp = ("ylo", "z")
    dp = ("x", "core")
    return jax.shard_map(
        body,
        mesh=fine,
        in_specs=(
            P(fsdp + ("yhi",), None, None),
            P(fsdp + ("yhi",), None, dp),
            P(fsdp + ("yhi",), None, None),
            P(fsdp + ("yhi",), None, dp),
            P(fsdp, dp + ("yhi",)),
            P(fsdp, dp + ("yhi",)),
            P(),
            P(None, dp),
            P(None, dp),
        ),
        out_specs=P(fsdp + ("yhi",), dp, None),
        check_vma=False,
    )
```

```python
import jax
import jax.numpy as jnp
from jax import lax
from jax.sharding import PartitionSpec as P

F32 = jnp.float32
BF16 = jnp.bfloat16

def shift(value, axis, step):
    size = lax.axis_size(axis)
    return lax.ppermute(value, axis, [(i, (i + step) % size) for i in range(size)])


def gathered(weight, piece, cot, early, inner_factor):
    barrier = lax.optimization_barrier
    n_z = lax.axis_size("z")
    z = lax.axis_index("z")
    half = weight.shape[0] // 2
    far_z = (z + n_z // 2) % n_z

    def up(value):
        return shift(value, "z", 1)

    def down(value):
        return shift(value, "z", -1)

    def across(value):
        return shift(value, "ylo", 1)

    def placed(result, by_offset):
        for offset, shard in by_offset:
            result = lax.dynamic_update_slice(result, shard[None], ((z + offset) % n_z, 0, 0))
        return result

    a1, b1, o0, w0, cot, piece, early = barrier(
        (up(weight), down(weight), across(weight), weight, cot, piece, early)
    )
    this_row = placed(
        jnp.zeros((n_z,) + weight.shape, weight.dtype), ((0, w0), (n_z - 1, a1))
    )
    a2, b2, here, o0, cot, own_factor, this_row = barrier(
        (
            up(a1),
            down(b1),
            shift(piece, "yhi", 1),
            o0,
            cot,
            inner_factor(early[0]),
            this_row,
        )
    )
    partner = lax.all_gather(here, ("x", "core"), axis=0, tiled=True)
    a3, b3, oa2, o0, b2 = barrier((up(a2), down(b2), across(a2), o0, b2))
    other_cot = shift(cot, "yhi", 1)
    oa1, ob1, ob2, a4, b4, oa2, other_cot = barrier(
        (up(o0), down(o0), across(b2), up(a3[:half]), down(b3[half:]), oa2, other_cot)
    )
    a4 = jnp.concatenate((a4, b4), axis=0)
    last = (
        (across(a4), far_z),
        (up(oa2), (z + n_z - 3) % n_z),
        (down(ob2), (z + 3) % n_z),
    )
    this_row = placed(
        this_row,
        ((1, b1), (n_z - 2, a2), (2, b2), (n_z - 3, a3), (3, b3), (n_z // 2, a4)),
    )
    other_row = placed(
        jnp.zeros_like(this_row),
        ((0, o0), (n_z - 1, oa1), (1, ob1), (n_z - 2, oa2), (2, ob2)),
    )
    flat = (n_z * weight.shape[0], -1)
    return this_row.reshape(flat), other_row.reshape(flat), last, other_cot, partner, early, own_factor


def projected(pre, cotangent, gate_projection, up_projection):
    cols = pre.shape[1] // 2
    gate = pre[:, :cols]
    up = pre[:, cols:]
    sigma = jax.nn.sigmoid(gate)
    upstream = cotangent.astype(F32)
    gate_grad = (upstream * up * sigma * (1.0 + gate * (1.0 - sigma))).astype(BF16)
    up_grad = (upstream * gate * sigma).astype(BF16)
    dims = (((1,), (1,)), ((), ()))
    return jnp.concatenate(
        (
            lax.dot_general(gate_projection, gate_grad, dims, preferred_element_type=F32),
            lax.dot_general(up_projection, up_grad, dims, preferred_element_type=F32),
        ),
        axis=0,
    )


def body(
    doc_inputs,
    doc_cotangents,
    query_inputs,
    query_cotangents,
    gate_weight,
    up_weight,
    input_projection,
    gate_projection,
    up_projection,
):
    count, length, width = doc_inputs.shape
    half_index = lax.axis_index("yhi")
    row_index = lax.axis_index("ylo")
    dq = ("x", "core", "yhi")
    fsdp = ("ylo", "z")
    n_dq = lax.axis_size(dq)
    n_fsdp = lax.axis_size(fsdp)
    rank = input_projection.shape[0]
    cols = gate_weight.shape[1]

    place = lax.axis_index(("x", "core"))
    piece = jnp.concatenate(
        (
            lax.dynamic_slice_in_dim(doc_inputs, place, 1, 0),
            lax.dynamic_slice_in_dim(query_inputs, place, 1, 0),
        ),
        axis=1,
    )
    own = jnp.concatenate((doc_inputs, query_inputs), axis=1)

    def columns(value, index):
        return lax.dynamic_slice_in_dim(value, index * cols, cols, value.ndim - 1)

    def cotangents(index):
        joined = jnp.concatenate(
            (columns(doc_cotangents, index), columns(query_cotangents, index)), axis=1
        )
        return joined.reshape(-1, cols)

    own_cot = cotangents(half_index)
    weight = jnp.concatenate((gate_weight, up_weight), axis=1)

    def inner_factor(rows):
        return lax.dot_general(
            rows.reshape(-1, width),
            input_projection,
            (((1,), (1,)), ((), ())),
            preferred_element_type=F32,
        )

    this_row, other_row, last, other_cot, other, (own, own_cot), own_factor = gathered(
        weight, piece, cotangents(1 - half_index), (own, own_cot), inner_factor
    )
    gate_proj = columns(gate_projection, half_index)
    up_proj = columns(up_projection, half_index)

    depth = this_row.shape[0]
    shard_depth = weight.shape[0]
    pres = []
    chunks = []
    for rows in (own, other):
        flat = rows.reshape(-1, width)
        this_flat = lax.dynamic_slice_in_dim(flat, row_index * depth, depth, 1)
        other_flat = lax.dynamic_slice_in_dim(flat, (1 - row_index) * depth, depth, 1)
        pre = jnp.dot(this_flat, this_row, preferred_element_type=F32)
        pres.append(pre + jnp.dot(other_flat, other_row, preferred_element_type=F32))
        chunks.append(
            [
                lax.dynamic_slice_in_dim(other_flat, place * shard_depth, shard_depth, 1)
                for _, place in last
            ]
        )
    shards = [shard for shard, _ in last]
    pres, own_factor, other, chunks, shards = lax.optimization_barrier(
        (pres, own_factor, other, chunks, shards)
    )
    factors = (own_factor, inner_factor(other))
    parts = []
    for pre, pieces, rows_cot in zip(pres, chunks, (own_cot, other_cot)):
        for chunk, shard in zip(pieces, shards):
            pre = pre + jnp.dot(chunk, shard, preferred_element_type=F32)
        parts.append(projected(pre, rows_cot, gate_proj, up_proj))

    first = half_index == 0

    def ordered(pair, axis):
        a = jnp.where(first, pair[0], pair[1])
        b = jnp.where(first, pair[1], pair[0])
        return jnp.concatenate((a, b), axis=axis)

    part = ordered(parts, 1).astype(BF16)
    in_factor = ordered(factors, 0)
    ranks = part.shape[0] // n_dq
    part = part.reshape(n_dq, ranks, -1)
    swapped = lax.all_to_all(part, dq, 0, 0, tiled=True)
    out_sum = jnp.sum(swapped.astype(F32), axis=0)

    pairs = 2 * count
    factor = jnp.einsum(
        "kel,elr->ekr",
        out_sum.reshape(ranks, 2 * pairs, length),
        in_factor.reshape(2 * pairs, length, rank),
        precision=lax.Precision.HIGHEST,
    ).reshape(pairs, 2, ranks * rank)
    docs = factor[:, 0]
    queries = factor[:, 1]
    doc_squares = jnp.sum(docs * docs, axis=1)
    docs = docs.astype(BF16)
    queries = queries.astype(BF16)

    everyone = lax.all_to_all(
        jnp.broadcast_to(queries[None], (n_fsdp,) + queries.shape), fsdp, 0, 0, tiled=True
    ).reshape(n_fsdp * pairs, -1)
    wide = everyone.astype(F32)
    query_squares = jnp.sum(wide * wide, axis=1)
    scores = lax.dot_general(
        docs, everyone, (((1,), (1,)), ((), ())), preferred_element_type=F32
    )
    total = scores.shape[1]

    def to_destinations(x):
        return x.reshape((2, count) + x.shape[1:]).swapaxes(0, 1).reshape(x.shape)

    payload = jnp.concatenate(
        (
            to_destinations(scores),
            jnp.broadcast_to(query_squares[None], (pairs, total)),
            jnp.broadcast_to(to_destinations(doc_squares)[:, None], (pairs, 128)),
        ),
        axis=1,
    )
    received = lax.all_to_all(payload, dq, 0, 0, tiled=True)
    sums = jnp.sum(received, axis=0)
    entries = 1.0 / (rank * 2 * rank)
    doc_scale = lax.rsqrt(sums[2 * total] * entries + 1e-06)
    query_scale = lax.rsqrt(sums[total : 2 * total] * entries + 1e-06)
    result = sums[:total] * query_scale * (doc_scale / rank)
    return result.reshape(1, 1, total)


def solution(mesh):
    fine = jax.sharding.Mesh(
        mesh.devices.reshape(2, mesh.shape["fsdp"] // 2, mesh.shape["dp"] // 2, 2, 2),
        ("ylo", "z", "x", "core", "yhi"),
    )
    fsdp = ("ylo", "z")
    dp = ("x", "core")
    return jax.shard_map(
        body,
        mesh=fine,
        in_specs=(
            P(fsdp + ("yhi",), None, None),
            P(fsdp + ("yhi",), None, dp),
            P(fsdp + ("yhi",), None, None),
            P(fsdp + ("yhi",), None, dp),
            P(fsdp, dp + ("yhi",)),
            P(fsdp, dp + ("yhi",)),
            P(),
            P(None, dp),
            P(None, dp),
        ),
        out_specs=P(fsdp + ("yhi",), dp, None),
        check_vma=False,
    )
```

```python
import jax
import jax.numpy as jnp
from jax import lax
from jax.sharding import PartitionSpec as P

F32 = jnp.float32
BF16 = jnp.bfloat16

def shift(value, axis, step):
    size = lax.axis_size(axis)
    return lax.ppermute(value, axis, [(i, (i + step) % size) for i in range(size)])


def gathered(weight, piece, cot, early, inner_factor):
    barrier = lax.optimization_barrier
    n_z = lax.axis_size("z")
    z = lax.axis_index("z")
    half = weight.shape[0] // 2
    far_z = (z + n_z // 2) % n_z

    def up(value):
        return shift(value, "z", 1)

    def down(value):
        return shift(value, "z", -1)

    def across(value):
        return shift(value, "ylo", 1)

    def placed(result, by_offset):
        for offset, shard in by_offset:
            result = lax.dynamic_update_slice(result, shard[None], ((z + offset) % n_z, 0, 0))
        return result

    a1, b1, o0, w0, cot, piece, early = barrier(
        (up(weight), down(weight), across(weight), weight, cot, piece, early)
    )
    this_row = placed(
        jnp.zeros((n_z,) + weight.shape, weight.dtype), ((0, w0), (n_z - 1, a1))
    )
    a2, b2, here, o0, cot, own_factor, this_row = barrier(
        (
            up(a1),
            down(b1),
            shift(piece, "yhi", 1),
            o0,
            cot,
            inner_factor(early[0]),
            this_row,
        )
    )
    partner = lax.all_gather(here, ("x", "core"), axis=0, tiled=True)
    a3, b3, oa2, o0, b2 = barrier((up(a2), down(b2), across(a2), o0, b2))
    other_cot = shift(cot, "yhi", 1)
    oa1, ob1, ob2, a4, b4, oa2, other_cot = barrier(
        (up(o0), down(o0), across(b2), up(a3[:half]), down(b3[half:]), oa2, other_cot)
    )
    a4 = jnp.concatenate((a4, b4), axis=0)
    last = (
        (across(a4), far_z),
        (up(oa2), (z + n_z - 3) % n_z),
        (down(ob2), (z + 3) % n_z),
    )
    this_row = placed(
        this_row,
        ((1, b1), (n_z - 2, a2), (2, b2), (n_z - 3, a3), (3, b3), (n_z // 2, a4)),
    )
    other_row = placed(
        jnp.zeros_like(this_row),
        ((0, o0), (n_z - 1, oa1), (1, ob1), (n_z - 2, oa2), (2, ob2)),
    )
    flat = (n_z * weight.shape[0], -1)
    return this_row.reshape(flat), other_row.reshape(flat), last, other_cot, partner, early, own_factor


def projected(pre, cotangent, gate_projection, up_projection):
    cols = pre.shape[1] // 2
    gate = pre[:, :cols]
    up = pre[:, cols:]
    sigma = jax.nn.sigmoid(gate)
    upstream = cotangent.astype(F32)
    gate_grad = (upstream * up * sigma * (1.0 + gate * (1.0 - sigma))).astype(BF16)
    up_grad = (upstream * gate * sigma).astype(BF16)
    dims = (((1,), (1,)), ((), ()))
    return jnp.concatenate(
        (
            lax.dot_general(gate_projection, gate_grad, dims, preferred_element_type=F32),
            lax.dot_general(up_projection, up_grad, dims, preferred_element_type=F32),
        ),
        axis=0,
    )


def body(
    doc_inputs,
    doc_cotangents,
    query_inputs,
    query_cotangents,
    gate_weight,
    up_weight,
    input_projection,
    gate_projection,
    up_projection,
):
    count, length, width = doc_inputs.shape
    half_index = lax.axis_index("yhi")
    row_index = lax.axis_index("ylo")
    dq = ("x", "core", "yhi")
    fsdp = ("ylo", "z")
    n_dq = lax.axis_size(dq)
    n_fsdp = lax.axis_size(fsdp)
    rank = input_projection.shape[0]
    cols = gate_weight.shape[1]

    place = lax.axis_index(("x", "core"))
    piece = jnp.concatenate(
        (
            lax.dynamic_slice_in_dim(doc_inputs, place, 1, 0),
            lax.dynamic_slice_in_dim(query_inputs, place, 1, 0),
        ),
        axis=1,
    )
    own = jnp.concatenate((doc_inputs, query_inputs), axis=1)

    def columns(value, index):
        return lax.dynamic_slice_in_dim(value, index * cols, cols, value.ndim - 1)

    def cotangents(index):
        joined = jnp.concatenate(
            (columns(doc_cotangents, index), columns(query_cotangents, index)), axis=1
        )
        return joined.reshape(-1, cols)

    own_cot = cotangents(half_index)
    weight = jnp.concatenate((gate_weight, up_weight), axis=1)

    def inner_factor(rows):
        return lax.dot_general(
            rows.reshape(-1, width),
            input_projection,
            (((1,), (1,)), ((), ())),
            preferred_element_type=F32,
        )

    this_row, other_row, last, other_cot, other, (own, own_cot), own_factor = gathered(
        weight, piece, cotangents(1 - half_index), (own, own_cot), inner_factor
    )
    gate_proj = columns(gate_projection, half_index)
    up_proj = columns(up_projection, half_index)

    depth = this_row.shape[0]
    shard_depth = weight.shape[0]
    pres = []
    chunks = []
    for rows in (own, other):
        flat = rows.reshape(-1, width)
        this_flat = lax.dynamic_slice_in_dim(flat, row_index * depth, depth, 1)
        other_flat = lax.dynamic_slice_in_dim(flat, (1 - row_index) * depth, depth, 1)
        pre = jnp.dot(this_flat, this_row, preferred_element_type=F32)
        pres.append(pre + jnp.dot(other_flat, other_row, preferred_element_type=F32))
        chunks.append(
            [
                lax.dynamic_slice_in_dim(other_flat, place * shard_depth, shard_depth, 1)
                for _, place in last
            ]
        )
    shards = [shard for shard, _ in last]
    pres, own_factor, other, chunks, shards = lax.optimization_barrier(
        (pres, own_factor, other, chunks, shards)
    )
    parts = []
    for pre, pieces, rows_cot in zip(pres, chunks, (own_cot, other_cot)):
        for chunk, shard in zip(pieces, shards):
            pre = pre + jnp.dot(chunk, shard, preferred_element_type=F32)
        parts.append(projected(pre, rows_cot, gate_proj, up_proj))

    first = half_index == 0

    def ordered(pair, axis):
        a = jnp.where(first, pair[0], pair[1])
        b = jnp.where(first, pair[1], pair[0])
        return jnp.concatenate((a, b), axis=axis)

    part = ordered(parts, 1).astype(BF16)
    part, other = lax.optimization_barrier((part, other))
    in_factor = ordered((own_factor, inner_factor(other)), 0)
    ranks = part.shape[0] // n_dq
    part = part.reshape(n_dq, ranks, -1)
    swapped = lax.all_to_all(part, dq, 0, 0, tiled=True)
    out_sum = jnp.sum(swapped.astype(F32), axis=0)

    pairs = 2 * count
    factor = jnp.einsum(
        "kel,elr->ekr",
        out_sum.reshape(ranks, 2 * pairs, length),
        in_factor.reshape(2 * pairs, length, rank),
        precision=lax.Precision.HIGHEST,
    ).reshape(pairs, 2, ranks * rank)
    docs = factor[:, 0]
    queries = factor[:, 1]
    doc_squares = jnp.sum(docs * docs, axis=1)
    docs = docs.astype(BF16)
    queries = queries.astype(BF16)

    everyone = lax.all_to_all(
        jnp.broadcast_to(queries[None], (n_fsdp,) + queries.shape), fsdp, 0, 0, tiled=True
    ).reshape(n_fsdp * pairs, -1)
    wide = everyone.astype(F32)
    query_squares = jnp.sum(wide * wide, axis=1)
    scores = lax.dot_general(
        docs, everyone, (((1,), (1,)), ((), ())), preferred_element_type=F32
    )
    total = scores.shape[1]

    def to_destinations(x):
        return x.reshape((2, count) + x.shape[1:]).swapaxes(0, 1).reshape(x.shape)

    payload = jnp.concatenate(
        (
            to_destinations(scores),
            jnp.broadcast_to(query_squares[None], (pairs, total)),
            jnp.broadcast_to(to_destinations(doc_squares)[:, None], (pairs, 128)),
        ),
        axis=1,
    )
    received = lax.all_to_all(payload, dq, 0, 0, tiled=True)
    sums = jnp.sum(received, axis=0)
    entries = 1.0 / (rank * 2 * rank)
    doc_scale = lax.rsqrt(sums[2 * total] * entries + 1e-06)
    query_scale = lax.rsqrt(sums[total : 2 * total] * entries + 1e-06)
    result = sums[:total] * query_scale * (doc_scale / rank)
    return result.reshape(1, 1, total)


def solution(mesh):
    fine = jax.sharding.Mesh(
        mesh.devices.reshape(2, mesh.shape["fsdp"] // 2, mesh.shape["dp"] // 2, 2, 2),
        ("ylo", "z", "x", "core", "yhi"),
    )
    fsdp = ("ylo", "z")
    dp = ("x", "core")
    return jax.shard_map(
        body,
        mesh=fine,
        in_specs=(
            P(fsdp + ("yhi",), None, None),
            P(fsdp + ("yhi",), None, dp),
            P(fsdp + ("yhi",), None, None),
            P(fsdp + ("yhi",), None, dp),
            P(fsdp, dp + ("yhi",)),
            P(fsdp, dp + ("yhi",)),
            P(),
            P(None, dp),
            P(None, dp),
        ),
        out_specs=P(fsdp + ("yhi",), dp, None),
        check_vma=False,
    )
```
